32 devices in a mesh: grp: 2 (over y), band: 16 (over z, x, core).
Axes of the slice: x: 2, y: 2, z: 4, core: 2. Of those that a mesh axis runs over, the one named last changes fastest.
Arguments:
- spec_in: bfloat16 [2, 64, 4656], P(None, 'grp', 'band'), parts along dimension 1, may hold values from -0.625 to 0.625
- forcing: bfloat16 [80, 2, 64, 5248], P('band', None, 'grp'), parts along dimension 2, may hold values from -6 to 6
- legendre: bfloat16 [4656, 80], P('band'), may hold values from -0.625 to 0.625
- weights: float32 [80], replicated, may hold values from 0.003 to 0.03
- cycle_slots: int32 [80], P('band'), may hold values from 0 to 79, each once
- wave_pairs: int32 [48], P('band'), may hold values from 0 to 47, each once
Outputs:
- grid_field: bfloat16 [80, 2, 64, 5248], P('band', None, 'grp'), parts along dimension 2
- spec_out: float32 [2, 64, 4656], P(None, 'grp', 'band'), parts along dimension 1
The draws below stay inside these ranges and needn't reach their ends.
There are 2 independent parts, one for each index of `grp`. The reference program is written for one: setup_inputs(seed, part) draws one part's arguments, and reference() takes and returns one part's arrays. A program takes and returns all parts, laid end to end along the dimension named above; an argument that names none is the same for every part. Nothing has to cross between parts.
Inputs may be any that keep to these rules, and one draw needn't show every extreme that they name: `cycle_slots`: each latitude once. `wave_pairs`: each pair once.
All inputs are finite; a program needn't handle non-finite values.
Results may differ from the reference program's by a relative error of at most 0.0072.
Values may be sent and summed in bfloat16 or wider, within the bound.
A program may use at most 128 MiB of HBM per device.

```python
import math
import jax
import jax.numpy as jnp
from jax import lax

TRUNC = 1279
NLON_EQ = 5136
NPAD = 5248
LEVELS = 32
MW = 96
SLOTS = 48
ROWS_ALL = 4656
LAT = 80


def block_levels(own_key, extent, pieces, least, high):
    factor_of, own = 1.0, jax.random.fold_in(own_key, 6)
    for axis_at, blocks in pieces:
        steps = jnp.exp(jax.random.uniform(jax.random.fold_in(own, axis_at), (blocks,), jnp.float32, least / len(pieces), high / len(pieces)))
        factor_of = factor_of * jnp.repeat(steps, extent[axis_at] // blocks).reshape([-1 if axis == axis_at else 1 for axis in range(len(extent))])
    return factor_of


def scatter_about(rng, dims, spread, bound, cuts=(), held_as=jnp.bfloat16):
    entries = jax.random.normal(rng, dims, jnp.float32) * spread
    if len(cuts) > 0:
        entries = block_levels(rng, dims, cuts, -0.22, 0.18) * entries
    return jnp.clip(entries, min=-bound, max=bound).astype(held_as)


def setup_inputs(seed: int = 0, part: int = 0) -> dict:
    keys = jax.random.split(jax.random.key(seed), 7)
    part_splits = jax.random.split(jax.random.fold_in(keys[6], part), 7)
    return {
        "spec_in": scatter_about(part_splits[0], (2, LEVELS, ROWS_ALL), MW ** -0.5, 0.625, ((2, 16),)),
        "forcing": scatter_about(part_splits[1], (LAT, 2, LEVELS, NPAD), 1.0, 6.0, ((0, 16),)),
        "legendre": scatter_about(keys[2], (ROWS_ALL, LAT), MW ** -0.5, 0.625, ((0, 16),)),
        "weights": jnp.clip(jnp.exp(jax.random.uniform(keys[3], (LAT,), jnp.float32, math.log(0.003), math.log(0.03))), 0.003, 0.03),
        "cycle_slots": jax.random.permutation(keys[4], LAT).astype(jnp.int32),
        "wave_pairs": jax.random.permutation(keys[5], SLOTS).astype(jnp.int32),
    }


two_pi = 2.0 * math.pi


def row_layout(pair_ids, window):
    offsets = jnp.arange(window + 1, dtype=jnp.int32)[None, :]
    boundary = window - pair_ids[:, None]
    second = offsets >= boundary
    degree_step = jnp.where(second, offsets - boundary, offsets)
    parity_sign = 1.0 - 2.0 * (degree_step % 2).astype(jnp.float32)
    return second.astype(jnp.float32), parity_sign


def wave_list(pair_ids, window):
    first_wave = TRUNC + 1 - window + pair_ids
    second_wave = TRUNC - pair_ids
    return jnp.stack([first_wave, second_wave], axis=1).reshape(-1).astype(jnp.int32)


def fourier_table(length, wave_numbers, points):
    blocks = points // 128
    high = jnp.arange(blocks, dtype=jnp.int32) * 128
    low = jnp.arange(128, dtype=jnp.int32)
    scale = two_pi / length.astype(jnp.float32)
    angle_high = ((wave_numbers[:, None] * high[None, :]) % length).astype(jnp.float32) * scale
    angle_low = ((wave_numbers[:, None] * low[None, :]) % length).astype(jnp.float32) * scale
    cos_high = jnp.cos(angle_high)[:, :, None]
    sin_high = jnp.sin(angle_high)[:, :, None]
    cos_low = jnp.cos(angle_low)[:, None, :]
    sin_low = jnp.sin(angle_low)[:, None, :]
    count = wave_numbers.shape[0]
    cosine = (cos_high * cos_low - sin_high * sin_low).reshape(count, points)
    minus_sine = (-(sin_high * cos_low + cos_high * sin_low)).reshape(count, points)
    inside = (jnp.arange(points, dtype=jnp.int32) < length)[None, :]
    cosine = jnp.where(inside, cosine, jnp.float32(0.0))
    minus_sine = jnp.where(inside, minus_sine, jnp.float32(0.0))
    return jnp.concatenate([cosine, minus_sine], axis=0).astype(jnp.bfloat16)


def reference(spec_in, forcing, legendre, weights, cycle_slots, wave_pairs):
    window = MW
    row_count = window + 1
    slot_count = wave_pairs.shape[0]
    level_count = spec_in.shape[1]
    lat_count = cycle_slots.shape[0]
    points = forcing.shape[3]
    second, parity_sign = row_layout(wave_pairs, window)
    belong = jnp.stack([1.0 - second, second], axis=1)
    signs_both = jnp.stack([jnp.ones_like(parity_sign), parity_sign], axis=1)
    coefficient = jnp.transpose(spec_in.reshape(2, level_count, slot_count, row_count), (2, 0, 1, 3))
    legendre_order = legendre.reshape(slot_count, row_count, lat_count)[:, :, cycle_slots]

    def invert_slot(packed):
        coef_slot, legendre_slot, belong_slot, sign_slot = packed
        masked_terms = coef_slot.astype(jnp.float32)[None, None] * belong_slot[None, :, None, None, :] * sign_slot[:, None, None, None, :]
        return jnp.einsum("hwelr,rq->hwelq", masked_terms, legendre_slot.astype(jnp.float32))

    fourier = lax.map(invert_slot, (coefficient, legendre_order, belong, signs_both)).astype(jnp.bfloat16)
    fourier = jnp.transpose(fourier, (5, 1, 4, 3, 0, 2)).reshape(lat_count, 2 * level_count, 2 * window)
    wave_numbers = wave_list(wave_pairs, window)
    lengths = (NLON_EQ - 4 * cycle_slots).astype(jnp.int32)
    force_rows = forcing.reshape(lat_count, 2 * level_count, points)

    def cycle_step(packed):
        fourier_cycle, force_cycle, length = packed
        dft_table = fourier_table(length, wave_numbers, points)
        field_rows = 2.0 * jnp.dot(fourier_cycle, dft_table, preferred_element_type=jnp.float32)
        product = (field_rows * force_cycle.astype(jnp.float32)).astype(jnp.bfloat16)
        returned = lax.dot_general(product, dft_table, (((1,), (1,)), ((), ())), preferred_element_type=jnp.float32)
        return field_rows.astype(jnp.bfloat16), returned.astype(jnp.bfloat16)

    fields, returned = lax.map(cycle_step, (fourier, force_rows, lengths))
    grid_field = fields.reshape(lat_count, 2, level_count, points)
    returned = returned.astype(jnp.float32).reshape(lat_count, 2, level_count, 2, slot_count, 2)
    north_part = returned[:, 0]
    south_part = returned[:, 1]
    lat_weight = weights[cycle_slots][:, None, None, None, None]
    combined = jnp.stack([lat_weight * (north_part + south_part), lat_weight * (north_part - south_part)]).astype(jnp.bfloat16)
    combined = jnp.transpose(combined, (4, 0, 1, 2, 3, 5))
    pick_parity = jnp.stack([parity_sign > 0, parity_sign < 0], axis=1).astype(jnp.float32)

    def direct_slot(packed):
        comb_slot, legendre_slot, belong_slot, pick_slot = packed
        values = jnp.einsum("pqlew,rq->plewr", comb_slot.astype(jnp.float32), legendre_slot.astype(jnp.float32))
        chosen = values * pick_slot[:, None, None, None, :] * belong_slot[None, None, None, :, :]
        return jnp.sum(chosen, axis=(0, 3))

    spectral = lax.map(direct_slot, (combined, legendre_order, belong, pick_parity))
    spec_out = jnp.transpose(spectral, (2, 1, 0, 3)).reshape(2, level_count, slot_count * row_count)
    return grid_field, spec_out
```

```python
import functools
import math

import jax
import jax.numpy as jnp
from jax import lax
from jax.experimental import pallas as pl
from jax.experimental.pallas import tpu as pltpu
from jax.sharding import PartitionSpec as P

TRUNC = 1279
NLON_EQ = 5136


two_pi = 2.0 * math.pi


def wave_list(pair_ids, window):
    first_wave = TRUNC + 1 - window + pair_ids
    second_wave = TRUNC - pair_ids
    return jnp.stack([first_wave, second_wave], axis=1).reshape(-1)


def fourier_table(length, wave_numbers, points):
    blocks = points // 128
    high = jnp.arange(blocks, dtype=jnp.int32) * 128
    low = jnp.arange(128, dtype=jnp.int32)
    scale = two_pi / length.astype(jnp.float32)
    angle_high = (wave_numbers[:, None] * high[None, :] % length).astype(jnp.float32) * scale
    angle_low = (wave_numbers[:, None] * low[None, :] % length).astype(jnp.float32) * scale
    cos_high = jnp.cos(angle_high)[:, :, None]
    sin_high = jnp.sin(angle_high)[:, :, None]
    cos_low = jnp.cos(angle_low)[:, None, :]
    sin_low = jnp.sin(angle_low)[:, None, :]
    count = wave_numbers.shape[0]
    cosine = (cos_high * cos_low - sin_high * sin_low).reshape(count, points)
    minus_sine = (-(sin_high * cos_low + cos_high * sin_low)).reshape(count, points)
    inside = (jnp.arange(points, dtype=jnp.int32) < length)[None, :]
    cosine = jnp.where(inside, cosine, jnp.float32(0.0))
    minus_sine = jnp.where(inside, minus_sine, jnp.float32(0.0))
    return jnp.concatenate([cosine, minus_sine], axis=0).astype(jnp.bfloat16)


def row_halves(array, axis):
    widths = [(0, 0)] * array.ndim
    widths[axis] = (0, 1)
    padded = jnp.pad(array, widths)
    shape = list(padded.shape)
    shape[axis : axis + 1] = [shape[axis] // 2, 2]
    folded = padded.reshape(shape)
    even_rows = lax.index_in_dim(folded, 0, axis + 1, keepdims=False)
    odd_rows = lax.index_in_dim(folded, 1, axis + 1, keepdims=False)
    return (even_rows, odd_rows)


def invert_rows(coefficient, legendre_rows, member, flip_sign, form):
    coef_even, coef_odd = row_halves(coefficient, 3)
    leg_even, leg_odd = row_halves(legendre_rows, 1)
    member_even, member_odd = row_halves(member, 1)
    stack_even = jnp.stack(
        [
            coef_even * (1.0 - member_even)[None, None].astype(jnp.bfloat16),
            coef_even * member_even[None, None].astype(jnp.bfloat16),
        ]
    )
    stack_odd = jnp.stack(
        [
            coef_odd * (1.0 - member_odd)[None, None].astype(jnp.bfloat16),
            coef_odd * member_odd[None, None].astype(jnp.bfloat16),
        ]
    )
    sum_even = jnp.einsum(form, stack_even, leg_even, preferred_element_type=jnp.float32)
    sum_odd = jnp.einsum(form, stack_odd, leg_odd, preferred_element_type=jnp.float32)
    north = sum_even + sum_odd
    south = (sum_even - sum_odd) * flip_sign[None, :, None, None, :]
    both = jnp.stack([north, south], axis=1)
    return jnp.transpose(both, (0, 1, 3, 4, 5, 2))


def direct_rows(combined, legendre_rows, member, flip_odd, form):
    leg_even, leg_odd = row_halves(legendre_rows, 1)
    member_even, member_odd = row_halves(member, 1)
    results = []
    for half, leg_half, member_half in ((0, leg_even, member_even), (1, leg_odd, member_odd)):
        first_part = combined[half, :, :, :, :, 0]
        second_part = jnp.where(
            flip_odd[None, None, None, :],
            combined[1 - half, :, :, :, :, 1],
            combined[half, :, :, :, :, 1],
        )
        stacked = jnp.stack([first_part, second_part])
        values = jnp.einsum(form, stacked, leg_half, preferred_element_type=jnp.float32)
        results.append(jnp.where(member_half[None, None] > 0.5, values[1], values[0]))
    merged = jnp.stack(results, axis=-1)
    shape = merged.shape
    merged = merged.reshape(shape[0], shape[1], shape[2], shape[3] * 2)
    return merged[:, :, :, : legendre_rows.shape[1]]


def on_device_wide(spec_in, forcing, legendre, weights, cycle_slots, wave_pairs):
    all_cycles, all_pairs = (
        lax.all_gather(cycle_slots, "band", axis=0, tiled=True),
        lax.all_gather(wave_pairs, "band", axis=0, tiled=True),
    )
    devices = lax.axis_size("band")
    slot_local = wave_pairs.shape[0]
    window = 2 * slot_local * devices
    row_count = window + 1
    level_count = spec_in.shape[1]
    lat_local = cycle_slots.shape[0]
    lat_count = all_cycles.shape[0]
    points = forcing.shape[3]
    offsets = jnp.arange(row_count, dtype=jnp.int32)[None, :]
    boundary = window - wave_pairs
    member = (offsets >= boundary[:, None]).astype(jnp.float32)
    flip_odd = boundary % 2 == 1
    flip_sign = jnp.stack(
        [jnp.ones((slot_local,), jnp.float32), jnp.where(flip_odd, -1.0, 1.0).astype(jnp.float32)]
    )
    coefficient = spec_in.reshape(2, level_count, slot_local, row_count)
    legendre_local = legendre.reshape(slot_local, row_count, lat_count)
    legendre_order = jnp.take(legendre_local, all_cycles, axis=2)
    fourier = invert_rows(
        coefficient, legendre_order, member, flip_sign, "welsr,srq->qwles"
    ).astype(jnp.bfloat16)
    received = lax.all_to_all(fourier, "band", split_axis=0, concat_axis=4, tiled=True)
    received = received.reshape(lat_local, 2 * level_count, 2 * window)
    wave_numbers = wave_list(all_pairs, window)
    lengths = NLON_EQ - 4 * cycle_slots
    force_rows = forcing.reshape(lat_local, 2 * level_count, points)

    def cycle_step(packed):
        fourier_cycle, force_cycle, length = packed
        dft_table = fourier_table(length, wave_numbers, points)
        field_rows = 2.0 * jnp.dot(fourier_cycle, dft_table, preferred_element_type=jnp.float32)
        product = (field_rows * force_cycle.astype(jnp.float32)).astype(jnp.bfloat16)
        returned = lax.dot_general(
            product, dft_table, (((1,), (1,)), ((), ())), preferred_element_type=jnp.float32
        )
        return (field_rows.astype(jnp.bfloat16), returned.astype(jnp.bfloat16))

    fields, returned = lax.map(cycle_step, (received, force_rows, lengths))
    grid_field = fields.reshape(lat_local, 2, level_count, points)
    returned = returned.reshape(lat_local, 2, level_count, 2, window // 2, 2)
    gathered = lax.all_to_all(returned, "band", split_axis=4, concat_axis=0, tiled=True).astype(
        jnp.float32
    )
    north_part = gathered[:, 0]
    south_part = gathered[:, 1]
    lat_weight = jnp.take(weights, all_cycles)[:, None, None, None, None]
    combined = jnp.stack(
        [lat_weight * (north_part + south_part), lat_weight * (north_part - south_part)]
    ).astype(jnp.bfloat16)
    spectral = direct_rows(combined, legendre_order, member, flip_odd, "wqles,srq->wlesr")
    spec_out = jnp.transpose(spectral, (1, 0, 2, 3)).reshape(2, level_count, slot_local * row_count)
    return (grid_field, spec_out)


MESH = pl.DeviceIdType.MESH
BLOCK = 256
GROUP = 16
LANES = 128


def unit_circle(steps, length, inverse):
    turns = jnp.floor(steps * inverse + 0.5)
    z = (steps - turns * length) * (inverse * math.pi)
    y = z * z
    s = -1.0 / 39916800.0
    for c in (1.0 / 362880.0, -1.0 / 5040.0, 1.0 / 120.0, -1.0 / 6.0, 1.0):
        s = s * y + c
    s = s * z
    k = 1.0 / 479001600.0
    for c in (-1.0 / 3628800.0, 1.0 / 40320.0, -1.0 / 720.0, 1.0 / 24.0, -0.5, 1.0):
        k = k * y + c
    return 1.0 - 2.0 * s * s, 2.0 * s * k


def fused_kernel(
    n, slots, lats, levels, lat_count, points,
    spec_ref, leg_ref, weights_ref, cyc_ref, pair_ref, force_hbm,
    field_hbm, out_ref,
    force_v, field_v, info, legm, coefm, send1, recv1, send2, recv2,
    pick, low, high_c, high_s, coef_z, back_z, twisted, prod,
    force_sem, field_sem, info_ss, info_rs, f_ss, f_rs, b_ss, b_rs,
):
    window = 2 * slots * n
    row_count = window + 1
    rows = slots * row_count
    base = TRUNC + 1 - window
    pairs = 2 * levels
    blocks = -(-points // BLOCK)
    whole = (NLON_EQ - 4 * (lat_count - 1)) // BLOCK
    f32, bf16, i32 = jnp.float32, jnp.bfloat16, jnp.int32
    me = lax.axis_index("band")
    part = lax.axis_index("grp")

    def force_copy(q):
        return pltpu.make_async_copy(force_hbm.at[q], force_v.at[q], force_sem.at[q])

    def field_copy(q):
        return pltpu.make_async_copy(field_v.at[q], field_hbm.at[q], field_sem.at[q])

    for q in range(lats):
        force_copy(q).start()

    barrier = pltpu.get_barrier_semaphore()

    def peer(i):
        return lax.rem(me + i, n)

    @pl.loop(1, n)
    def _(i):
        pl.semaphore_signal(barrier, inc=1, device_id=(part, peer(i)), device_id_type=MESH)

    row16 = lax.broadcasted_iota(i32, (GROUP, LANES), 0)
    mine = jnp.full((GROUP, LANES), -1, i32)
    for q in range(lats):
        for s in range(slots):
            mine = jnp.where(row16 == q * slots + s, cyc_ref[q] * 65536 + pair_ref[s], mine)
    info[me] = mine

    def remote(src, dst, ssem, rsem, to, frm):
        return pltpu.make_async_remote_copy(
            src_ref=src, dst_ref=dst, send_sem=ssem.at[to], recv_sem=rsem.at[frm],
            device_id=(part, to), device_id_type=MESH,
        )

    pl.semaphore_wait(barrier, n - 1)

    @pl.loop(1, n)
    def _(i):
        remote(info.at[me], info.at[me], info_ss, info_rs, peer(i), me).start()

    @pl.loop(0, lats)
    def _(q):
        length = jnp.full((1, LANES), NLON_EQ - 4 * cyc_ref[q], i32).astype(f32)
        inverse = 1.0 / length
        m_low = base + lax.broadcasted_iota(i32, (BLOCK, LANES), 1)
        v_low = lax.broadcasted_iota(i32, (BLOCK, LANES), 0)
        c, s = unit_circle((m_low * v_low).astype(f32), length, inverse)
        low[q, :, 0:LANES] = c.astype(bf16)
        low[q, :, LANES : 2 * LANES] = s.astype(bf16)
        height = high_c.shape[1]
        m_high = base + lax.broadcasted_iota(i32, (height, LANES), 1)
        u_high = lax.broadcasted_iota(i32, (height, LANES), 0) * BLOCK
        c, s = unit_circle((m_high * u_high).astype(f32), length, inverse)
        high_c[q] = c
        high_s[q] = s

    lane = lax.broadcasted_iota(i32, (1, rows), 1)
    offset = lane
    boundary = jnp.full((1, rows), 0, i32) + (window - pair_ref[0])
    for s in range(1, slots):
        here = lane >= s * row_count
        offset = jnp.where(here, lane - s * row_count, offset)
        boundary = jnp.where(here, window - pair_ref[s], boundary)
    second = offset >= boundary
    odd = (jnp.where(second, offset - boundary, offset) & 1) == 1
    in_wave = [jnp.where(second, 0.0, 1.0), jnp.where(second, 1.0, 0.0)]
    sign = jnp.where(odd, -1.0, 1.0)
    for w in range(2):
        for e in range(2):
            part_we = spec_ref[e].astype(f32) * in_wave[w]
            at = (w * 2 + e) * pairs
            coefm[at : at + levels, :] = part_we.astype(bf16)
            coefm[at + levels : at + pairs, :] = (part_we * sign).astype(bf16)

    @pl.loop(1, n)
    def _(i):
        frm = lax.rem(me + n - i, n)
        remote(info.at[frm], info.at[frm], info_ss, info_rs, peer(i), frm).wait_recv()

    total = n * GROUP
    gathered = info[...].reshape(total, LANES)
    cycles = gathered >> 16
    waves = gathered & 65535
    hot = jnp.where(cycles == lax.broadcasted_iota(i32, (total, LANES), 1), 1.0, 0.0)
    leg_all = lax.dot_general(
        hot[:, :lat_count].astype(bf16), leg_ref[...], (((1,), (1,)), ((), ())),
        preferred_element_type=f32,
    )

    def row_lat(width):
        place = lax.broadcasted_iota(i32, (total, width), 0) & (GROUP - 1)
        lat = jnp.zeros((total, width), i32)
        for k in range(1, GROUP // slots + 1):
            lat = lat + jnp.where(place >= k * slots, 1, 0)
        return lat, place - lat * slots

    _, slot_of = row_lat(rows)
    lane_full = lax.broadcasted_iota(i32, (total, rows), 1) - slot_of * row_count
    keep = (lane_full >= 0) & (lane_full < row_count)
    legm[...] = jnp.where(keep, leg_all, 0.0).astype(bf16)
    fourier = lax.dot_general(
        legm[...], coefm[...], (((1,), (1,)), ((), ())), preferred_element_type=f32
    ).astype(bf16)
    send1[...] = fourier.reshape(n, GROUP, 4 * pairs)

    @pl.loop(1, n)
    def _(i):
        remote(send1.at[peer(i)], recv1.at[me], f_ss, f_rs, peer(i), me).start()

    recv1[me] = send1[me]
    lat_of, _ = row_lat(LANES)
    lane128 = lax.broadcasted_iota(i32, (total, LANES), 1)
    for q in range(lats):
        here = lat_of == q
        pick[0, q] = jnp.where(here & (lane128 == waves), 1.0, 0.0).astype(bf16)
        pick[1, q] = jnp.where(here & (lane128 == window - 1 - waves), 1.0, 0.0).astype(bf16)

    @pl.loop(1, n)
    def _(i):
        frm = lax.rem(me + n - i, n)
        remote(send1.at[peer(i)], recv1.at[frm], f_ss, f_rs, peer(i), frm).wait_recv()

    half = 2 * pairs
    arrived = recv1[...].reshape(total, 2 * half)
    for q in range(lats):
        z = jnp.zeros((half, LANES), f32)
        for w in range(2):
            z = z + lax.dot_general(
                arrived[:, w * half : (w + 1) * half], pick[w, q], (((0,), (0,)), ((), ())),
                preferred_element_type=f32,
            )
        coef_z[q] = 2.0 * z

    per = twisted.shape[0] // pairs

    @pl.loop(0, lats)
    def _(q):
        force_copy(q).wait()
        length = NLON_EQ - 4 * cyc_ref[q]
        acc_re = jnp.zeros((pairs, LANES), f32)
        acc_im = jnp.zeros((pairs, LANES), f32)
        for first in range(0, blocks, per):
            count = min(per, blocks - first)
            size = count * pairs
            real = coef_z[q, 0:pairs]
            imag = coef_z[q, pairs:half]
            for k in range(count):
                u = first + k
                hc = high_c[q, u : u + 1, :]
                hs = high_s[q, u : u + 1, :]
                twisted[k * pairs : (k + 1) * pairs, 0:LANES] = (real * hc - imag * hs).astype(bf16)
                twisted[k * pairs : (k + 1) * pairs, LANES : 2 * LANES] = (
                    -(real * hs + imag * hc)
                ).astype(bf16)
            fields = lax.dot_general(
                twisted[0:size], low[q], (((1,), (1,)), ((), ())), preferred_element_type=f32
            )
            for k in range(count):
                u = first + k
                width = min(BLOCK, points - u * BLOCK)
                f = fields[k * pairs : (k + 1) * pairs, 0:width]
                if u >= whole:
                    j = u * BLOCK + lax.broadcasted_iota(i32, (pairs, width), 1)
                    f = jnp.where(j < length, f, 0.0)
                field_v[q, :, u * BLOCK : u * BLOCK + width] = f.astype(bf16)
                p = f * force_v[q, :, u * BLOCK : u * BLOCK + width].astype(f32)
                prod[k * pairs : (k + 1) * pairs, 0:width] = p.astype(bf16)
                if width < BLOCK:
                    prod[k * pairs : (k + 1) * pairs, width:BLOCK] = jnp.zeros(
                        (pairs, BLOCK - width), bf16
                    )
            back = jnp.dot(prod[0:size], low[q], preferred_element_type=f32)
            for k in range(count):
                u = first + k
                hc = high_c[q, u : u + 1, :]
                hs = high_s[q, u : u + 1, :]
                tc = back[k * pairs : (k + 1) * pairs, 0:LANES]
                ts = back[k * pairs : (k + 1) * pairs, LANES : 2 * LANES]
                acc_re = acc_re + (tc * hc - ts * hs)
                acc_im = acc_im - (tc * hs + ts * hc)
        field_copy(q).start()
        weight = weights_ref[cyc_ref[q]]
        for e, acc in ((0, acc_re), (1, acc_im)):
            rounded = acc.astype(bf16).astype(f32)
            north = rounded[0:levels]
            south = rounded[levels:pairs]
            back_z[q, e * pairs : e * pairs + levels] = (weight * (north + south)).astype(bf16)
            back_z[q, e * pairs + levels : (e + 1) * pairs] = (weight * (north - south)).astype(bf16)

    for w in range(2):
        z = jnp.zeros((total, half), f32)
        for q in range(lats):
            z = z + lax.dot_general(
                pick[w, q], back_z[q], (((1,), (1,)), ((), ())), preferred_element_type=f32
            )
        send2[:, :, w * half : (w + 1) * half] = z.astype(bf16).reshape(n, GROUP, half)

    @pl.loop(1, n)
    def _(i):
        remote(send2.at[peer(i)], recv2.at[me], b_ss, b_rs, peer(i), me).start()

    recv2[me] = send2[me]

    @pl.loop(1, n)
    def _(i):
        frm = lax.rem(me + n - i, n)
        remote(send2.at[peer(i)], recv2.at[frm], b_ss, b_rs, peer(i), frm).wait_recv()

    final = lax.dot_general(
        recv2[...].reshape(total, 2 * half), legm[...], (((0,), (0,)), ((), ())),
        preferred_element_type=f32,
    )
    for e in range(2):
        chosen = []
        for w in range(2):
            at = (w * 2 + e) * pairs
            chosen.append(
                jnp.where(odd, final[at + levels : at + pairs], final[at : at + levels])
            )
        out_ref[e] = jnp.where(second, chosen[1], chosen[0])

    @pl.loop(1, n)
    def _(i):
        to = peer(i)
        remote(info.at[me], info.at[me], info_ss, info_rs, to, me).wait_send()
        remote(send1.at[to], recv1.at[me], f_ss, f_rs, to, me).wait_send()
        remote(send2.at[to], recv2.at[me], b_ss, b_rs, to, me).wait_send()

    for q in range(lats):
        field_copy(q).wait()


def on_device(n, spec_in, forcing, legendre, weights, cycle_slots, wave_pairs):
    slots = wave_pairs.shape[0]
    lats = cycle_slots.shape[0]
    levels = spec_in.shape[1]
    rows, lat_count = legendre.shape
    points = forcing.shape[3]
    pairs = 2 * levels
    half = 2 * pairs
    total = n * GROUP
    blocks = -(-points // BLOCK)
    per = 7
    bf16, f32 = jnp.bfloat16, jnp.float32
    vmem = pl.BlockSpec(memory_space=pltpu.VMEM)
    smem = pl.BlockSpec(memory_space=pltpu.SMEM)
    hbm = pl.BlockSpec(memory_space=pl.ANY)
    dma = pltpu.SemaphoreType.DMA
    high_rows = -(-blocks // 8) * 8
    field, spec_out = pl.pallas_call(
        functools.partial(fused_kernel, n, slots, lats, levels, lat_count, points),
        out_shape=(
            jax.ShapeDtypeStruct((lats, pairs, points), bf16),
            jax.ShapeDtypeStruct((2, levels, rows), f32),
        ),
        in_specs=[vmem, vmem, smem, smem, smem, hbm],
        out_specs=(hbm, vmem),
        scratch_shapes=[
            pltpu.VMEM((lats, pairs, points), bf16),
            pltpu.VMEM((lats, pairs, points), bf16),
            pltpu.VMEM((n, GROUP, LANES), jnp.int32),
            pltpu.VMEM((total, rows), bf16),
            pltpu.VMEM((2 * half, rows), bf16),
            pltpu.VMEM((n, GROUP, 2 * half), bf16),
            pltpu.VMEM((n, GROUP, 2 * half), bf16),
            pltpu.VMEM((n, GROUP, 2 * half), bf16),
            pltpu.VMEM((n, GROUP, 2 * half), bf16),
            pltpu.VMEM((2, lats, total, LANES), bf16),
            pltpu.VMEM((lats, BLOCK, 2 * LANES), bf16),
            pltpu.VMEM((lats, high_rows, LANES), f32),
            pltpu.VMEM((lats, high_rows, LANES), f32),
            pltpu.VMEM((lats, half, LANES), f32),
            pltpu.VMEM((lats, half, LANES), bf16),
            pltpu.VMEM((per * pairs, 2 * LANES), bf16),
            pltpu.VMEM((per * pairs, 2 * LANES), bf16),
            dma((lats,)), dma((lats,)),
            dma((n,)), dma((n,)), dma((n,)), dma((n,)), dma((n,)), dma((n,)),
        ],
        compiler_params=pltpu.CompilerParams(
            collective_id=0, has_side_effects=True, vmem_limit_bytes=48 * 1024 * 1024
        ),
    )(spec_in, legendre, weights, cycle_slots, wave_pairs, forcing.reshape(lats, pairs, points))
    return field.reshape(lats, 2, levels, points), spec_out


def solution(mesh):
    n = mesh.shape["band"]

    def run(spec_in, forcing, legendre, weights, cycle_slots, wave_pairs):
        slots = wave_pairs.shape[0]
        narrow = (
            2 * slots * n <= LANES
            and legendre.shape[1] <= LANES
            and slots * cycle_slots.shape[0] <= GROUP
            and spec_in.shape[1] % 32 == 0
        )
        args = (spec_in, forcing, legendre, weights, cycle_slots, wave_pairs)
        return on_device(n, *args) if narrow else on_device_wide(*args)

    in_specs = (
        P(None, "grp", "band"),
        P("band", None, "grp", None),
        P("band", None),
        P(),
        P("band"),
        P("band"),
    )
    out_specs = (P("band", None, "grp", None), P(None, "grp", "band"))
    return jax.shard_map(
        run, mesh=mesh, in_specs=in_specs, out_specs=out_specs, check_vma=False
    )
```

```python
import functools
import math

import jax
import jax.numpy as jnp
from jax import lax
from jax.experimental import pallas as pl
from jax.experimental.pallas import tpu as pltpu
from jax.sharding import PartitionSpec as P

TRUNC = 1279
NLON_EQ = 5136


two_pi = 2.0 * math.pi


def wave_list(pair_ids, window):
    first_wave = TRUNC + 1 - window + pair_ids
    second_wave = TRUNC - pair_ids
    return jnp.stack([first_wave, second_wave], axis=1).reshape(-1)


def fourier_table(length, wave_numbers, points):
    blocks = points // 128
    high = jnp.arange(blocks, dtype=jnp.int32) * 128
    low = jnp.arange(128, dtype=jnp.int32)
    scale = two_pi / length.astype(jnp.float32)
    angle_high = (wave_numbers[:, None] * high[None, :] % length).astype(jnp.float32) * scale
    angle_low = (wave_numbers[:, None] * low[None, :] % length).astype(jnp.float32) * scale
    cos_high = jnp.cos(angle_high)[:, :, None]
    sin_high = jnp.sin(angle_high)[:, :, None]
    cos_low = jnp.cos(angle_low)[:, None, :]
    sin_low = jnp.sin(angle_low)[:, None, :]
    count = wave_numbers.shape[0]
    cosine = (cos_high * cos_low - sin_high * sin_low).reshape(count, points)
    minus_sine = (-(sin_high * cos_low + cos_high * sin_low)).reshape(count, points)
    inside = (jnp.arange(points, dtype=jnp.int32) < length)[None, :]
    cosine = jnp.where(inside, cosine, jnp.float32(0.0))
    minus_sine = jnp.where(inside, minus_sine, jnp.float32(0.0))
    return jnp.concatenate([cosine, minus_sine], axis=0).astype(jnp.bfloat16)


def row_halves(array, axis):
    widths = [(0, 0)] * array.ndim
    widths[axis] = (0, 1)
    padded = jnp.pad(array, widths)
    shape = list(padded.shape)
    shape[axis : axis + 1] = [shape[axis] // 2, 2]
    folded = padded.reshape(shape)
    even_rows = lax.index_in_dim(folded, 0, axis + 1, keepdims=False)
    odd_rows = lax.index_in_dim(folded, 1, axis + 1, keepdims=False)
    return (even_rows, odd_rows)


def invert_rows(coefficient, legendre_rows, member, flip_sign, form):
    coef_even, coef_odd = row_halves(coefficient, 3)
    leg_even, leg_odd = row_halves(legendre_rows, 1)
    member_even, member_odd = row_halves(member, 1)
    stack_even = jnp.stack(
        [
            coef_even * (1.0 - member_even)[None, None].astype(jnp.bfloat16),
            coef_even * member_even[None, None].astype(jnp.bfloat16),
        ]
    )
    stack_odd = jnp.stack(
        [
            coef_odd * (1.0 - member_odd)[None, None].astype(jnp.bfloat16),
            coef_odd * member_odd[None, None].astype(jnp.bfloat16),
        ]
    )
    sum_even = jnp.einsum(form, stack_even, leg_even, preferred_element_type=jnp.float32)
    sum_odd = jnp.einsum(form, stack_odd, leg_odd, preferred_element_type=jnp.float32)
    north = sum_even + sum_odd
    south = (sum_even - sum_odd) * flip_sign[None, :, None, None, :]
    both = jnp.stack([north, south], axis=1)
    return jnp.transpose(both, (0, 1, 3, 4, 5, 2))


def direct_rows(combined, legendre_rows, member, flip_odd, form):
    leg_even, leg_odd = row_halves(legendre_rows, 1)
    member_even, member_odd = row_halves(member, 1)
    results = []
    for half, leg_half, member_half in ((0, leg_even, member_even), (1, leg_odd, member_odd)):
        first_part = combined[half, :, :, :, :, 0]
        second_part = jnp.where(
            flip_odd[None, None, None, :],
            combined[1 - half, :, :, :, :, 1],
            combined[half, :, :, :, :, 1],
        )
        stacked = jnp.stack([first_part, second_part])
        values = jnp.einsum(form, stacked, leg_half, preferred_element_type=jnp.float32)
        results.append(jnp.where(member_half[None, None] > 0.5, values[1], values[0]))
    merged = jnp.stack(results, axis=-1)
    shape = merged.shape
    merged = merged.reshape(shape[0], shape[1], shape[2], shape[3] * 2)
    return merged[:, :, :, : legendre_rows.shape[1]]


def on_device_wide(spec_in, forcing, legendre, weights, cycle_slots, wave_pairs):
    all_cycles, all_pairs = (
        lax.all_gather(cycle_slots, "band", axis=0, tiled=True),
        lax.all_gather(wave_pairs, "band", axis=0, tiled=True),
    )
    devices = lax.axis_size("band")
    slot_local = wave_pairs.shape[0]
    window = 2 * slot_local * devices
    row_count = window + 1
    level_count = spec_in.shape[1]
    lat_local = cycle_slots.shape[0]
    lat_count = all_cycles.shape[0]
    points = forcing.shape[3]
    offsets = jnp.arange(row_count, dtype=jnp.int32)[None, :]
    boundary = window - wave_pairs
    member = (offsets >= boundary[:, None]).astype(jnp.float32)
    flip_odd = boundary % 2 == 1
    flip_sign = jnp.stack(
        [jnp.ones((slot_local,), jnp.float32), jnp.where(flip_odd, -1.0, 1.0).astype(jnp.float32)]
    )
    coefficient = spec_in.reshape(2, level_count, slot_local, row_count)
    legendre_local = legendre.reshape(slot_local, row_count, lat_count)
    legendre_order = jnp.take(legendre_local, all_cycles, axis=2)
    fourier = invert_rows(
        coefficient, legendre_order, member, flip_sign, "welsr,srq->qwles"
    ).astype(jnp.bfloat16)
    received = lax.all_to_all(fourier, "band", split_axis=0, concat_axis=4, tiled=True)
    received = received.reshape(lat_local, 2 * level_count, 2 * window)
    wave_numbers = wave_list(all_pairs, window)
    lengths = NLON_EQ - 4 * cycle_slots
    force_rows = forcing.reshape(lat_local, 2 * level_count, points)

    def cycle_step(packed):
        fourier_cycle, force_cycle, length = packed
        dft_table = fourier_table(length, wave_numbers, points)
        field_rows = 2.0 * jnp.dot(fourier_cycle, dft_table, preferred_element_type=jnp.float32)
        product = (field_rows * force_cycle.astype(jnp.float32)).astype(jnp.bfloat16)
        returned = lax.dot_general(
            product, dft_table, (((1,), (1,)), ((), ())), preferred_element_type=jnp.float32
        )
        return (field_rows.astype(jnp.bfloat16), returned.astype(jnp.bfloat16))

    fields, returned = lax.map(cycle_step, (received, force_rows, lengths))
    grid_field = fields.reshape(lat_local, 2, level_count, points)
    returned = returned.reshape(lat_local, 2, level_count, 2, window // 2, 2)
    gathered = lax.all_to_all(returned, "band", split_axis=4, concat_axis=0, tiled=True).astype(
        jnp.float32
    )
    north_part = gathered[:, 0]
    south_part = gathered[:, 1]
    lat_weight = jnp.take(weights, all_cycles)[:, None, None, None, None]
    combined = jnp.stack(
        [lat_weight * (north_part + south_part), lat_weight * (north_part - south_part)]
    ).astype(jnp.bfloat16)
    spectral = direct_rows(combined, legendre_order, member, flip_odd, "wqles,srq->wlesr")
    spec_out = jnp.transpose(spectral, (1, 0, 2, 3)).reshape(2, level_count, slot_local * row_count)
    return (grid_field, spec_out)


MESH = pl.DeviceIdType.MESH
BLOCK = 256
GROUP = 16
CHUNKS = 1
PER = 21
LANES = 128


def unit_circle(steps, length, inverse):
    turns = jnp.floor(steps * inverse + 0.5)
    z = (steps - turns * length) * (inverse * math.pi)
    y = z * z
    s = -1.0 / 39916800.0
    for c in (1.0 / 362880.0, -1.0 / 5040.0, 1.0 / 120.0, -1.0 / 6.0, 1.0):
        s = s * y + c
    s = s * z
    k = 1.0 / 479001600.0
    for c in (-1.0 / 3628800.0, 1.0 / 40320.0, -1.0 / 720.0, 1.0 / 24.0, -0.5, 1.0):
        k = k * y + c
    return 1.0 - 2.0 * s * s, 2.0 * s * k


def fused_kernel(
    n, slots, lats, levels, lat_count, points,
    spec_hbm, leg_hbm, weights_hbm, cyc_hbm, pair_hbm, force_hbm,
    field_v, out_ref,
    spec_ref, leg_ref, weights_ref, cyc_ref, pair_ref, small_sem, force_v, info, legm, coefm, send1, recv1, send2, recv2,
    pick, low, high_c, high_s, coef_z, back_z, twisted, prod,
    force_sem, info_ss, info_rs, f_ss, f_rs, b_ss, b_rs,
):
    window = 2 * slots * n
    row_count = window + 1
    rows = slots * row_count
    base = TRUNC + 1 - window
    chunks = send1.shape[0]
    part_levels = levels // chunks
    pairs = 2 * part_levels
    half = 2 * pairs
    blocks = -(-points // BLOCK)
    whole = (NLON_EQ - 4 * (lat_count - 1)) // BLOCK
    f32, bf16, i32 = jnp.float32, jnp.bfloat16, jnp.int32
    me = lax.axis_index("band")
    part = lax.axis_index("grp")

    def force_copy(q):
        return pltpu.make_async_copy(force_hbm.at[q], force_v.at[q], force_sem.at[q])

    small = [
        pltpu.make_async_copy(a, b, small_sem.at[i])
        for i, (a, b) in enumerate(
            (
                (cyc_hbm, cyc_ref),
                (pair_hbm, pair_ref),
                (spec_hbm, spec_ref),
                (leg_hbm, leg_ref),
                (weights_hbm, weights_ref),
            )
        )
    ]
    for copy in small:
        copy.start()

    barrier = pltpu.get_barrier_semaphore()

    def peer(i):
        return lax.rem(me + i, n)

    @pl.loop(1, n)
    def _(i):
        pl.semaphore_signal(barrier, inc=1, device_id=(part, peer(i)), device_id_type=MESH)

    for q in range(lats):
        force_copy(q).start()
    small[0].wait()
    small[1].wait()

    lane1 = lax.broadcasted_iota(i32, (1, LANES), 1)
    mine = jnp.full((1, LANES), -1.0, f32)
    for q in range(lats):
        for s in range(slots):
            k = q * slots + s
            mine = jnp.where(lane1 == k, cyc_ref[q].astype(f32), mine)
            mine = jnp.where(lane1 == GROUP + k, pair_ref[s].astype(f32), mine)
    info[me] = mine

    def remote(src, dst, ssem, rsem, to):
        return pltpu.make_async_remote_copy(
            src_ref=src, dst_ref=dst, send_sem=ssem, recv_sem=rsem,
            device_id=(part, to), device_id_type=MESH,
        )

    def all_of(buffer, sem):
        others = buffer.at[pl.ds(0, n - 1)]
        return pltpu.make_async_copy(others, others, sem)

    pl.semaphore_wait(barrier, n - 1)

    @pl.loop(1, n)
    def _(i):
        remote(info.at[me], info.at[me], info_ss.at[0], info_rs.at[0], peer(i)).start()

    @pl.loop(0, lats)
    def _(q):
        length = jnp.full((1, LANES), NLON_EQ - 4 * cyc_ref[q], i32).astype(f32)
        inverse = 1.0 / length
        m_low = base + lax.broadcasted_iota(i32, (BLOCK, LANES), 1)
        v_low = lax.broadcasted_iota(i32, (BLOCK, LANES), 0)
        c, s = unit_circle((m_low * v_low).astype(f32), length, inverse)
        low[q, :, 0:LANES] = c.astype(bf16)
        low[q, :, LANES : 2 * LANES] = s.astype(bf16)
        height = high_c.shape[1]
        m_high = base + lax.broadcasted_iota(i32, (height, LANES), 1)
        u_high = lax.broadcasted_iota(i32, (height, LANES), 0) * BLOCK
        c, s = unit_circle((m_high * u_high).astype(f32), length, inverse)
        high_c[q] = c
        high_s[q] = s

    for copy in small[2:]:
        copy.wait()

    lane = lax.broadcasted_iota(i32, (1, rows), 1)
    offset = lane
    boundary = jnp.full((1, rows), 0, i32) + (window - pair_ref[0])
    for s in range(1, slots):
        here = lane >= s * row_count
        offset = jnp.where(here, lane - s * row_count, offset)
        boundary = jnp.where(here, window - pair_ref[s], boundary)
    second = offset >= boundary
    odd = (jnp.where(second, offset - boundary, offset) & 1) == 1
    in_wave = [jnp.where(second, 0.0, 1.0), jnp.where(second, 1.0, 0.0)]
    sign = jnp.where(odd, -1.0, 1.0)
    for e in range(2):
        values = spec_ref[e].astype(f32)
        for w in range(2):
            north = values * in_wave[w]
            south = north * sign
            for c in range(chunks):
                at = c * 2 * half + (w * 2 + e) * pairs
                take = slice(c * part_levels, (c + 1) * part_levels)
                coefm[at : at + part_levels, :] = north[take].astype(bf16)
                coefm[at + part_levels : at + pairs, :] = south[take].astype(bf16)
    back_z[...] = jnp.zeros_like(back_z)
    all_of(info, info_rs.at[0]).wait()

    total = n * GROUP
    gathered = jnp.broadcast_to(info[...], (n, GROUP, LANES)).reshape(total, LANES)
    lane_all = lax.broadcasted_iota(i32, (total, LANES), 1)
    place_all = lax.broadcasted_iota(i32, (total, LANES), 0) & (GROUP - 1)

    def column(first):
        here = lane_all == place_all + first
        return jnp.sum(jnp.where(here, gathered, 0.0), axis=1, keepdims=True).astype(i32)

    cycles = column(0)
    waves = column(GROUP)
    hot = jnp.where(cycles == lax.broadcasted_iota(i32, (total, LANES), 1), 1.0, 0.0)
    leg_all = lax.dot_general(
        hot[:, :lat_count].astype(bf16), leg_ref[...], (((1,), (0,)), ((), ())),
        preferred_element_type=f32,
    )

    def row_lat(width):
        place = lax.broadcasted_iota(i32, (total, width), 0) & (GROUP - 1)
        lat = jnp.zeros((total, width), i32)
        for k in range(1, GROUP // slots + 1):
            lat = lat + jnp.where(place >= k * slots, 1, 0)
        return lat, place - lat * slots

    _, slot_of = row_lat(rows)
    lane_full = lax.broadcasted_iota(i32, (total, rows), 1) - slot_of * row_count
    keep = (lane_full >= 0) & (lane_full < row_count)
    legm[...] = jnp.where(keep, leg_all, 0.0).astype(bf16)
    fourier = lax.dot_general(
        legm[...], coefm[...], (((1,), (1,)), ((), ())), preferred_element_type=f32
    ).astype(bf16)
    for c in range(chunks):
        send1[c] = fourier[:, c * 2 * half : (c + 1) * 2 * half].reshape(n, GROUP, 2 * half)

    for c in range(chunks):

        @pl.loop(1, n)
        def _(i):
            to = peer(i)
            remote(send1.at[c, to], recv1.at[c, me], f_ss.at[c], f_rs.at[c], to).start()

        recv1[c, me] = send1[c, me]

    lat_of, _ = row_lat(LANES)
    for q in range(lats):
        here = lat_of == q
        at = q * 2 * LANES
        pick[:, at : at + LANES] = jnp.where(here & (lane_all == waves), 1.0, 0.0).astype(bf16)
        pick[:, at + LANES : at + 2 * LANES] = jnp.where(
            here & (lane_all == window - 1 - waves), 1.0, 0.0
        ).astype(bf16)

    per = twisted.shape[0] // pairs
    for c in range(chunks):

        all_of(recv1.at[c], f_rs.at[c]).wait()

        arrived = recv1[c].reshape(total, 2 * half)
        both = lax.dot_general(
            arrived, pick[...], (((0,), (0,)), ((), ())), preferred_element_type=f32
        )
        for q in range(lats):
            at = q * 2 * LANES
            coef_z[c, q] = 2.0 * (
                both[0:half, at : at + LANES] + both[half : 2 * half, at + LANES : at + 2 * LANES]
            )

        @pl.loop(0, lats)
        def _(q):
            if c == 0:
                force_copy(q).wait()
            length = NLON_EQ - 4 * cyc_ref[q]
            acc_re = jnp.zeros((pairs, LANES), f32)
            acc_im = jnp.zeros((pairs, LANES), f32)
            for first in range(0, blocks, per):
                count = min(per, blocks - first)
                fields = low_sums(coef_z, high_c, high_s, low, twisted, (c, q), q, pairs, first, count)
                for k in range(count):
                    u = first + k
                    width = min(BLOCK, points - u * BLOCK)
                    f = inside(fields[k * pairs : (k + 1) * pairs, 0:width], u, whole, length)
                    cols = slice(u * BLOCK, u * BLOCK + width)
                    for h in range(2):
                        rows_h = slice(h * levels + c * part_levels, h * levels + (c + 1) * part_levels)
                        at = k * pairs + h * part_levels
                        fh = f[h * part_levels : (h + 1) * part_levels]
                        field_v[q, rows_h, cols] = fh.astype(bf16)
                        p = fh * force_v[q, rows_h, cols].astype(f32)
                        prod[at : at + part_levels, 0:width] = p.astype(bf16)
                    if width < BLOCK:
                        prod[k * pairs : (k + 1) * pairs, width:BLOCK] = jnp.zeros(
                            (pairs, BLOCK - width), bf16
                        )
                back = jnp.dot(prod[0 : count * pairs], low[q], preferred_element_type=f32)
                for k in range(count):
                    u = first + k
                    hc = high_c[q, u : u + 1, :]
                    hs = high_s[q, u : u + 1, :]
                    tc = back[k * pairs : (k + 1) * pairs, 0:LANES]
                    ts = back[k * pairs : (k + 1) * pairs, LANES : 2 * LANES]
                    acc_re = acc_re + (tc * hc - ts * hs)
                    acc_im = acc_im - (tc * hs + ts * hc)
            weight = weights_ref[cyc_ref[q]]
            for e, acc in ((0, acc_re), (1, acc_im)):
                rounded = acc.astype(bf16).astype(f32)
                north = rounded[0:part_levels]
                south = rounded[part_levels:pairs]
                for g, value in ((0, north + south), (1, north - south)):
                    value = (weight * value).astype(bf16)
                    for w in range(2):
                        at = w * half + e * pairs + g * part_levels
                        lane_at = pl.multiple_of(q * 2 * LANES + w * LANES, LANES)
                        back_z[at : at + part_levels, pl.ds(lane_at, LANES)] = value

        z = lax.dot_general(
            pick[...], back_z[...], (((1,), (1,)), ((), ())), preferred_element_type=f32
        )
        send2[c] = z.astype(bf16).reshape(n, GROUP, 2 * half)

        @pl.loop(1, n)
        def _(i):
            to = peer(i)
            remote(send2.at[c, to], recv2.at[c, me], b_ss.at[c], b_rs.at[c], to).start()

        recv2[c, me] = send2[c, me]

    for c in range(chunks):

        all_of(recv2.at[c], b_rs.at[c]).wait()

        final = lax.dot_general(
            recv2[c].reshape(total, 2 * half), legm[...], (((0,), (0,)), ((), ())),
            preferred_element_type=f32,
        )
        for e in range(2):
            chosen = []
            for w in range(2):
                at = (w * 2 + e) * pairs
                chosen.append(
                    jnp.where(odd, final[at + part_levels : at + pairs], final[at : at + part_levels])
                )
            out_ref[e, c * part_levels : (c + 1) * part_levels] = jnp.where(second, chosen[1], chosen[0])

    all_of(info, info_ss.at[0]).wait()
    for c in range(chunks):
        all_of(send1.at[c], f_ss.at[c]).wait()
        all_of(send2.at[c], b_ss.at[c]).wait()


def low_sums(coef_z, high_c, high_s, low, twisted, at, q, pairs, first, count):
    real = coef_z[at[0], at[1], 0:pairs]
    imag = coef_z[at[0], at[1], pairs : 2 * pairs]
    for k in range(count):
        hc = high_c[q, first + k : first + k + 1, :]
        hs = high_s[q, first + k : first + k + 1, :]
        rows = slice(k * pairs, (k + 1) * pairs)
        twisted[rows, 0:LANES] = (real * hc - imag * hs).astype(jnp.bfloat16)
        twisted[rows, LANES : 2 * LANES] = (-(real * hs + imag * hc)).astype(jnp.bfloat16)
    return lax.dot_general(
        twisted[0 : count * pairs], low[q], (((1,), (1,)), ((), ())),
        preferred_element_type=jnp.float32,
    )


def inside(f, u, whole, length):
    if u < whole:
        return f
    j = u * BLOCK + lax.broadcasted_iota(jnp.int32, f.shape, 1)
    return jnp.where(j < length, f, 0.0)


def on_device(n, spec_in, forcing, legendre, weights, cycle_slots, wave_pairs):
    slots = wave_pairs.shape[0]
    lats = cycle_slots.shape[0]
    levels = spec_in.shape[1]
    rows, lat_count = legendre.shape
    points = forcing.shape[3]
    chunks = CHUNKS
    pairs = 2 * levels // chunks
    half = 2 * pairs
    total = n * GROUP
    blocks = -(-points // BLOCK)
    per = PER
    bf16, f32 = jnp.bfloat16, jnp.float32
    vmem = pl.BlockSpec(memory_space=pltpu.VMEM)
    hbm = pl.BlockSpec(memory_space=pltpu.HBM)
    dma = pltpu.SemaphoreType.DMA
    high_rows = -(-blocks // 8) * 8
    coef_shape = (chunks, lats, half, LANES)
    low_shape = (lats, BLOCK, 2 * LANES)
    high_shape = (lats, high_rows, LANES)
    message = pltpu.VMEM((chunks, n, GROUP, 2 * half), bf16)
    field, spec_out = pl.pallas_call(
        functools.partial(fused_kernel, n, slots, lats, levels, lat_count, points),
        out_shape=(
            jax.ShapeDtypeStruct((lats, 2 * levels, points), bf16),
            jax.ShapeDtypeStruct((2, levels, rows), f32),
        ),
        in_specs=[hbm] * 6,
        out_specs=(vmem, vmem),
        scratch_shapes=[
            pltpu.VMEM((2, levels, rows), bf16),
            pltpu.VMEM((lat_count, rows), bf16),
            pltpu.SMEM((lat_count,), f32),
            pltpu.SMEM((lats,), jnp.int32),
            pltpu.SMEM((slots,), jnp.int32),
            dma((5,)),
            pltpu.VMEM((lats, 2 * levels, points), bf16),
            pltpu.VMEM((n, 1, LANES), f32),
            pltpu.VMEM((total, rows), bf16),
            pltpu.VMEM((chunks * 2 * half, rows), bf16),
            message, message, message, message,
            pltpu.VMEM((total, lats * 2 * LANES), bf16),
            pltpu.VMEM(low_shape, bf16),
            pltpu.VMEM(high_shape, f32),
            pltpu.VMEM(high_shape, f32),
            pltpu.VMEM(coef_shape, f32),
            pltpu.VMEM((2 * half, lats * 2 * LANES), bf16),
            pltpu.VMEM((per * pairs, 2 * LANES), bf16),
            pltpu.VMEM((per * pairs, 2 * LANES), bf16),
            dma((lats,)), dma((1,)), dma((1,)),
            dma((chunks,)), dma((chunks,)), dma((chunks,)), dma((chunks,)),
        ],
        compiler_params=pltpu.CompilerParams(
            collective_id=0, has_side_effects=True,
            vmem_limit_bytes=49 * 1024 * 1024 + 512 * 1024,
        ),
    )(
        spec_in, legendre.T, weights, cycle_slots, wave_pairs,
        forcing.reshape(lats, 2 * levels, points),
    )
    return field.reshape(lats, 2, levels, points), spec_out


def solution(mesh):
    n = mesh.shape["band"]

    def run(spec_in, forcing, legendre, weights, cycle_slots, wave_pairs):
        slots = wave_pairs.shape[0]
        narrow = (
            2 * slots * n <= LANES
            and legendre.shape[1] <= LANES
            and slots * cycle_slots.shape[0] <= GROUP
            and spec_in.shape[1] % 32 == 0
        )
        args = (spec_in, forcing, legendre, weights, cycle_slots, wave_pairs)
        return on_device(n, *args) if narrow else on_device_wide(*args)

    in_specs = (
        P(None, "grp", "band"),
        P("band", None, "grp", None),
        P("band", None),
        P(),
        P("band"),
        P("band"),
    )
    out_specs = (P("band", None, "grp", None), P(None, "grp", "band"))
    return jax.shard_map(
        run, mesh=mesh, in_specs=in_specs, out_specs=out_specs, check_vma=False
    )
```

```python
import functools
import math

import jax
import jax.numpy as jnp
from jax import lax
from jax.experimental import pallas as pl
from jax.experimental.pallas import tpu as pltpu
from jax.sharding import PartitionSpec as P

TRUNC = 1279
NLON_EQ = 5136


two_pi = 2.0 * math.pi


def wave_list(pair_ids, window):
    first_wave = TRUNC + 1 - window + pair_ids
    second_wave = TRUNC - pair_ids
    return jnp.stack([first_wave, second_wave], axis=1).reshape(-1)


def fourier_table(length, wave_numbers, points):
    blocks = points // 128
    high = jnp.arange(blocks, dtype=jnp.int32) * 128
    low = jnp.arange(128, dtype=jnp.int32)
    scale = two_pi / length.astype(jnp.float32)
    angle_high = (wave_numbers[:, None] * high[None, :] % length).astype(jnp.float32) * scale
    angle_low = (wave_numbers[:, None] * low[None, :] % length).astype(jnp.float32) * scale
    cos_high = jnp.cos(angle_high)[:, :, None]
    sin_high = jnp.sin(angle_high)[:, :, None]
    cos_low = jnp.cos(angle_low)[:, None, :]
    sin_low = jnp.sin(angle_low)[:, None, :]
    count = wave_numbers.shape[0]
    cosine = (cos_high * cos_low - sin_high * sin_low).reshape(count, points)
    minus_sine = (-(sin_high * cos_low + cos_high * sin_low)).reshape(count, points)
    inside = (jnp.arange(points, dtype=jnp.int32) < length)[None, :]
    cosine = jnp.where(inside, cosine, jnp.float32(0.0))
    minus_sine = jnp.where(inside, minus_sine, jnp.float32(0.0))
    return jnp.concatenate([cosine, minus_sine], axis=0).astype(jnp.bfloat16)


def row_halves(array, axis):
    widths = [(0, 0)] * array.ndim
    widths[axis] = (0, 1)
    padded = jnp.pad(array, widths)
    shape = list(padded.shape)
    shape[axis : axis + 1] = [shape[axis] // 2, 2]
    folded = padded.reshape(shape)
    even_rows = lax.index_in_dim(folded, 0, axis + 1, keepdims=False)
    odd_rows = lax.index_in_dim(folded, 1, axis + 1, keepdims=False)
    return (even_rows, odd_rows)


def invert_rows(coefficient, legendre_rows, member, flip_sign, form):
    coef_even, coef_odd = row_halves(coefficient, 3)
    leg_even, leg_odd = row_halves(legendre_rows, 1)
    member_even, member_odd = row_halves(member, 1)
    stack_even = jnp.stack(
        [
            coef_even * (1.0 - member_even)[None, None].astype(jnp.bfloat16),
            coef_even * member_even[None, None].astype(jnp.bfloat16),
        ]
    )
    stack_odd = jnp.stack(
        [
            coef_odd * (1.0 - member_odd)[None, None].astype(jnp.bfloat16),
            coef_odd * member_odd[None, None].astype(jnp.bfloat16),
        ]
    )
    sum_even = jnp.einsum(form, stack_even, leg_even, preferred_element_type=jnp.float32)
    sum_odd = jnp.einsum(form, stack_odd, leg_odd, preferred_element_type=jnp.float32)
    north = sum_even + sum_odd
    south = (sum_even - sum_odd) * flip_sign[None, :, None, None, :]
    both = jnp.stack([north, south], axis=1)
    return jnp.transpose(both, (0, 1, 3, 4, 5, 2))


def direct_rows(combined, legendre_rows, member, flip_odd, form):
    leg_even, leg_odd = row_halves(legendre_rows, 1)
    member_even, member_odd = row_halves(member, 1)
    results = []
    for half, leg_half, member_half in ((0, leg_even, member_even), (1, leg_odd, member_odd)):
        first_part = combined[half, :, :, :, :, 0]
        second_part = jnp.where(
            flip_odd[None, None, None, :],
            combined[1 - half, :, :, :, :, 1],
            combined[half, :, :, :, :, 1],
        )
        stacked = jnp.stack([first_part, second_part])
        values = jnp.einsum(form, stacked, leg_half, preferred_element_type=jnp.float32)
        results.append(jnp.where(member_half[None, None] > 0.5, values[1], values[0]))
    merged = jnp.stack(results, axis=-1)
    shape = merged.shape
    merged = merged.reshape(shape[0], shape[1], shape[2], shape[3] * 2)
    return merged[:, :, :, : legendre_rows.shape[1]]


def on_device_wide(spec_in, forcing, legendre, weights, cycle_slots, wave_pairs):
    all_cycles, all_pairs = (
        lax.all_gather(cycle_slots, "band", axis=0, tiled=True),
        lax.all_gather(wave_pairs, "band", axis=0, tiled=True),
    )
    devices = lax.axis_size("band")
    slot_local = wave_pairs.shape[0]
    window = 2 * slot_local * devices
    row_count = window + 1
    level_count = spec_in.shape[1]
    lat_local = cycle_slots.shape[0]
    lat_count = all_cycles.shape[0]
    points = forcing.shape[3]
    offsets = jnp.arange(row_count, dtype=jnp.int32)[None, :]
    boundary = window - wave_pairs
    member = (offsets >= boundary[:, None]).astype(jnp.float32)
    flip_odd = boundary % 2 == 1
    flip_sign = jnp.stack(
        [jnp.ones((slot_local,), jnp.float32), jnp.where(flip_odd, -1.0, 1.0).astype(jnp.float32)]
    )
    coefficient = spec_in.reshape(2, level_count, slot_local, row_count)
    legendre_local = legendre.reshape(slot_local, row_count, lat_count)
    legendre_order = jnp.take(legendre_local, all_cycles, axis=2)
    fourier = invert_rows(
        coefficient, legendre_order, member, flip_sign, "welsr,srq->qwles"
    ).astype(jnp.bfloat16)
    received = lax.all_to_all(fourier, "band", split_axis=0, concat_axis=4, tiled=True)
    received = received.reshape(lat_local, 2 * level_count, 2 * window)
    wave_numbers = wave_list(all_pairs, window)
    lengths = NLON_EQ - 4 * cycle_slots
    force_rows = forcing.reshape(lat_local, 2 * level_count, points)

    def cycle_step(packed):
        fourier_cycle, force_cycle, length = packed
        dft_table = fourier_table(length, wave_numbers, points)
        field_rows = 2.0 * jnp.dot(fourier_cycle, dft_table, preferred_element_type=jnp.float32)
        product = (field_rows * force_cycle.astype(jnp.float32)).astype(jnp.bfloat16)
        returned = lax.dot_general(
            product, dft_table, (((1,), (1,)), ((), ())), preferred_element_type=jnp.float32
        )
        return (field_rows.astype(jnp.bfloat16), returned.astype(jnp.bfloat16))

    fields, returned = lax.map(cycle_step, (received, force_rows, lengths))
    grid_field = fields.reshape(lat_local, 2, level_count, points)
    returned = returned.reshape(lat_local, 2, level_count, 2, window // 2, 2)
    gathered = lax.all_to_all(returned, "band", split_axis=4, concat_axis=0, tiled=True).astype(
        jnp.float32
    )
    north_part = gathered[:, 0]
    south_part = gathered[:, 1]
    lat_weight = jnp.take(weights, all_cycles)[:, None, None, None, None]
    combined = jnp.stack(
        [lat_weight * (north_part + south_part), lat_weight * (north_part - south_part)]
    ).astype(jnp.bfloat16)
    spectral = direct_rows(combined, legendre_order, member, flip_odd, "wqles,srq->wlesr")
    spec_out = jnp.transpose(spectral, (1, 0, 2, 3)).reshape(2, level_count, slot_local * row_count)
    return (grid_field, spec_out)


MESH = pl.DeviceIdType.MESH
BLOCK = 256
GROUP = 16
CHUNKS = 1
PER = 21
LANES = 128


def unit_circle(steps, length, inverse):
    turns = jnp.floor(steps * inverse + 0.5)
    z = (steps - turns * length) * (inverse * math.pi)
    y = z * z
    s = -1.0 / 39916800.0
    for c in (1.0 / 362880.0, -1.0 / 5040.0, 1.0 / 120.0, -1.0 / 6.0, 1.0):
        s = s * y + c
    s = s * z
    k = 1.0 / 479001600.0
    for c in (-1.0 / 3628800.0, 1.0 / 40320.0, -1.0 / 720.0, 1.0 / 24.0, -0.5, 1.0):
        k = k * y + c
    return 1.0 - 2.0 * s * s, 2.0 * s * k


def fused_kernel(
    n, slots, lats, levels, lat_count, points,
    table_ref, facts_ref, weights_ref, force_hbm,
    field_v, out_ref,
    force_v, info, legm, coefm, send1, recv1, send2, recv2,
    pick, low, high_c, high_s, coef_z, back_z, twisted, prod,
    force_sem, info_ss, info_rs, f_ss, f_rs, b_ss, b_rs,
):
    window = 2 * slots * n
    row_count = window + 1
    rows = slots * row_count
    base = TRUNC + 1 - window
    chunks = send1.shape[0]
    part_levels = levels // chunks
    pairs = 2 * part_levels
    half = 2 * pairs
    blocks = -(-points // BLOCK)
    whole = (NLON_EQ - 4 * (lat_count - 1)) // BLOCK
    f32, bf16, i32 = jnp.float32, jnp.bfloat16, jnp.int32
    me = lax.axis_index("band")
    part = lax.axis_index("grp")

    def force_copy(q):
        return pltpu.make_async_copy(force_hbm.at[q], force_v.at[q], force_sem.at[q])

    def cycle(q):
        return facts_ref[0, LANES + q]

    def pair(s):
        return facts_ref[0, LANES + lats + s]

    barrier = pltpu.get_barrier_semaphore()

    def peer(i):
        return lax.rem(me + i, n)

    @pl.loop(1, n)
    def _(i):
        pl.semaphore_signal(barrier, inc=1, device_id=(part, peer(i)), device_id_type=MESH)

    for q in range(lats):
        force_copy(q).start()

    lane1 = lax.broadcasted_iota(i32, (1, LANES), 1)
    mine = jnp.full((1, LANES), -1.0, f32)
    for q in range(lats):
        for s in range(slots):
            k = q * slots + s
            mine = jnp.where(lane1 == k, cycle(q), mine)
            mine = jnp.where(lane1 == GROUP + k, pair(s), mine)
    info[me] = mine

    def remote(src, dst, ssem, rsem, to):
        return pltpu.make_async_remote_copy(
            src_ref=src, dst_ref=dst, send_sem=ssem, recv_sem=rsem,
            device_id=(part, to), device_id_type=MESH,
        )

    def all_of(buffer, sem):
        others = buffer.at[pl.ds(0, n - 1)]
        return pltpu.make_async_copy(others, others, sem)

    pl.semaphore_wait(barrier, n - 1)

    @pl.loop(1, n)
    def _(i):
        remote(info.at[me], info.at[me], info_ss.at[0], info_rs.at[0], peer(i)).start()

    @pl.loop(0, lats)
    def _(q):
        length = jnp.full((1, LANES), NLON_EQ - 4.0 * cycle(q), f32)
        inverse = 1.0 / length
        m_low = base + lax.broadcasted_iota(i32, (BLOCK, LANES), 1)
        v_low = lax.broadcasted_iota(i32, (BLOCK, LANES), 0)
        c, s = unit_circle((m_low * v_low).astype(f32), length, inverse)
        low[q, :, 0:LANES] = c.astype(bf16)
        low[q, :, LANES : 2 * LANES] = s.astype(bf16)
        height = high_c.shape[1]
        m_high = base + lax.broadcasted_iota(i32, (height, LANES), 1)
        u_high = lax.broadcasted_iota(i32, (height, LANES), 0) * BLOCK
        c, s = unit_circle((m_high * u_high).astype(f32), length, inverse)
        high_c[q] = c
        high_s[q] = s

    lane = lax.broadcasted_iota(i32, (1, rows), 1).astype(f32)
    offset = lane
    boundary = jnp.full((1, rows), window - pair(0), f32)
    for s in range(1, slots):
        here = lane >= s * row_count
        offset = jnp.where(here, lane - s * row_count, offset)
        boundary = jnp.where(here, window - pair(s), boundary)
    second = offset >= boundary
    degree = jnp.where(second, offset - boundary, offset)
    odd = degree - 2.0 * jnp.floor(0.5 * degree) > 0.5
    in_wave = [jnp.where(second, 0.0, 1.0), jnp.where(second, 1.0, 0.0)]
    sign = jnp.where(odd, -1.0, 1.0)
    for e in range(2):
        values = table_ref[e * levels : (e + 1) * levels].astype(f32)
        for w in range(2):
            north = values * in_wave[w]
            south = north * sign
            for c in range(chunks):
                at = c * 2 * half + (w * 2 + e) * pairs
                take = slice(c * part_levels, (c + 1) * part_levels)
                coefm[at : at + part_levels, :] = north[take].astype(bf16)
                coefm[at + part_levels : at + pairs, :] = south[take].astype(bf16)
    back_z[...] = jnp.zeros_like(back_z)
    all_of(info, info_rs.at[0]).wait()

    total = n * GROUP
    gathered = jnp.broadcast_to(info[...], (n, GROUP, LANES)).reshape(total, LANES)
    lane_all = lax.broadcasted_iota(i32, (total, LANES), 1)
    place_all = lax.broadcasted_iota(i32, (total, LANES), 0) & (GROUP - 1)

    def column(first):
        here = lane_all == place_all + first
        return jnp.sum(jnp.where(here, gathered, 0.0), axis=1, keepdims=True).astype(i32)

    cycles = column(0)
    waves = column(GROUP)
    hot = jnp.where(cycles == lax.broadcasted_iota(i32, (total, LANES), 1), 1.0, 0.0)
    leg_all = lax.dot_general(
        hot[:, :lat_count].astype(bf16), table_ref[2 * levels : 2 * levels + lat_count], (((1,), (0,)), ((), ())),
        preferred_element_type=f32,
    )

    def row_lat(width):
        place = lax.broadcasted_iota(i32, (total, width), 0) & (GROUP - 1)
        lat = jnp.zeros((total, width), i32)
        for k in range(1, GROUP // slots + 1):
            lat = lat + jnp.where(place >= k * slots, 1, 0)
        return lat, place - lat * slots

    _, slot_of = row_lat(rows)
    lane_full = lax.broadcasted_iota(i32, (total, rows), 1) - slot_of * row_count
    keep = (lane_full >= 0) & (lane_full < row_count)
    legm[...] = jnp.where(keep, leg_all, 0.0).astype(bf16)
    fourier = lax.dot_general(
        legm[...], coefm[...], (((1,), (1,)), ((), ())), preferred_element_type=f32
    ).astype(bf16)
    for c in range(chunks):
        send1[c] = fourier[:, c * 2 * half : (c + 1) * 2 * half].reshape(n, GROUP, 2 * half)

    for c in range(chunks):

        @pl.loop(1, n)
        def _(i):
            to = peer(i)
            remote(send1.at[c, to], recv1.at[c, me], f_ss.at[c], f_rs.at[c], to).start()

        recv1[c, me] = send1[c, me]

    lat_of, _ = row_lat(LANES)
    for q in range(lats):
        here = lat_of == q
        at = q * 2 * LANES
        pick[:, at : at + LANES] = jnp.where(here & (lane_all == waves), 1.0, 0.0).astype(bf16)
        pick[:, at + LANES : at + 2 * LANES] = jnp.where(
            here & (lane_all == window - 1 - waves), 1.0, 0.0
        ).astype(bf16)

    per = twisted.shape[0] // pairs
    for c in range(chunks):

        all_of(recv1.at[c], f_rs.at[c]).wait()

        arrived = recv1[c].reshape(total, 2 * half)
        both = lax.dot_general(
            arrived, pick[...], (((0,), (0,)), ((), ())), preferred_element_type=f32
        )
        for q in range(lats):
            at = q * 2 * LANES
            coef_z[c, q] = 2.0 * (
                both[0:half, at : at + LANES] + both[half : 2 * half, at + LANES : at + 2 * LANES]
            )

        @pl.loop(0, lats)
        def _(q):
            if c == 0:
                force_copy(q).wait()
            length = NLON_EQ - 4.0 * cycle(q)
            acc_re = jnp.zeros((pairs, LANES), f32)
            acc_im = jnp.zeros((pairs, LANES), f32)
            for first in range(0, blocks, per):
                count = min(per, blocks - first)
                fields = low_sums(coef_z, high_c, high_s, low, twisted, (c, q), q, pairs, first, count)
                for k in range(count):
                    u = first + k
                    width = min(BLOCK, points - u * BLOCK)
                    f = inside(fields[k * pairs : (k + 1) * pairs, 0:width], u, whole, length)
                    cols = slice(u * BLOCK, u * BLOCK + width)
                    for h in range(2):
                        rows_h = slice(h * levels + c * part_levels, h * levels + (c + 1) * part_levels)
                        at = k * pairs + h * part_levels
                        fh = f[h * part_levels : (h + 1) * part_levels]
                        field_v[q, rows_h, cols] = fh.astype(bf16)
                        p = fh * force_v[q, rows_h, cols].astype(f32)
                        prod[at : at + part_levels, 0:width] = p.astype(bf16)
                    if width < BLOCK:
                        prod[k * pairs : (k + 1) * pairs, width:BLOCK] = jnp.zeros(
                            (pairs, BLOCK - width), bf16
                        )
                back = jnp.dot(prod[0 : count * pairs], low[q], preferred_element_type=f32)
                for k in range(count):
                    u = first + k
                    hc = high_c[q, u : u + 1, :]
                    hs = high_s[q, u : u + 1, :]
                    tc = back[k * pairs : (k + 1) * pairs, 0:LANES]
                    ts = back[k * pairs : (k + 1) * pairs, LANES : 2 * LANES]
                    acc_re = acc_re + (tc * hc - ts * hs)
                    acc_im = acc_im - (tc * hs + ts * hc)
            mine = lax.broadcasted_iota(i32, (1, LANES), 1).astype(f32) == cycle(q)
            weight = jnp.sum(
                jnp.where(mine, weights_ref[:, 0:LANES], 0.0), axis=1, keepdims=True
            )
            for e, acc in ((0, acc_re), (1, acc_im)):
                rounded = acc.astype(bf16).astype(f32)
                north = rounded[0:part_levels]
                south = rounded[part_levels:pairs]
                for g, value in ((0, north + south), (1, north - south)):
                    value = (weight * value).astype(bf16)
                    for w in range(2):
                        at = w * half + e * pairs + g * part_levels
                        lane_at = pl.multiple_of(q * 2 * LANES + w * LANES, LANES)
                        back_z[at : at + part_levels, pl.ds(lane_at, LANES)] = value

        z = lax.dot_general(
            pick[...], back_z[...], (((1,), (1,)), ((), ())), preferred_element_type=f32
        )
        send2[c] = z.astype(bf16).reshape(n, GROUP, 2 * half)

        @pl.loop(1, n)
        def _(i):
            to = peer(i)
            remote(send2.at[c, to], recv2.at[c, me], b_ss.at[c], b_rs.at[c], to).start()

        recv2[c, me] = send2[c, me]

    for c in range(chunks):

        all_of(recv2.at[c], b_rs.at[c]).wait()

        final = lax.dot_general(
            recv2[c].reshape(total, 2 * half), legm[...], (((0,), (0,)), ((), ())),
            preferred_element_type=f32,
        )
        for e in range(2):
            chosen = []
            for w in range(2):
                at = (w * 2 + e) * pairs
                chosen.append(
                    jnp.where(odd, final[at + part_levels : at + pairs], final[at : at + part_levels])
                )
            out_ref[e, c * part_levels : (c + 1) * part_levels] = jnp.where(second, chosen[1], chosen[0])

    all_of(info, info_ss.at[0]).wait()
    for c in range(chunks):
        all_of(send1.at[c], f_ss.at[c]).wait()
        all_of(send2.at[c], b_ss.at[c]).wait()


def low_sums(coef_z, high_c, high_s, low, twisted, at, q, pairs, first, count):
    real = coef_z[at[0], at[1], 0:pairs]
    imag = coef_z[at[0], at[1], pairs : 2 * pairs]
    for k in range(count):
        hc = high_c[q, first + k : first + k + 1, :]
        hs = high_s[q, first + k : first + k + 1, :]
        rows = slice(k * pairs, (k + 1) * pairs)
        twisted[rows, 0:LANES] = (real * hc - imag * hs).astype(jnp.bfloat16)
        twisted[rows, LANES : 2 * LANES] = (-(real * hs + imag * hc)).astype(jnp.bfloat16)
    return lax.dot_general(
        twisted[0 : count * pairs], low[q], (((1,), (1,)), ((), ())),
        preferred_element_type=jnp.float32,
    )


def inside(f, u, whole, length):
    if u < whole:
        return f
    j = u * BLOCK + lax.broadcasted_iota(jnp.int32, f.shape, 1)
    return jnp.where(j.astype(jnp.float32) < length, f, 0.0)


def on_device(n, spec_in, forcing, legendre, weights, cycle_slots, wave_pairs):
    slots = wave_pairs.shape[0]
    lats = cycle_slots.shape[0]
    levels = spec_in.shape[1]
    rows, lat_count = legendre.shape
    points = forcing.shape[3]
    chunks = CHUNKS
    pairs = 2 * levels // chunks
    half = 2 * pairs
    total = n * GROUP
    blocks = -(-points // BLOCK)
    per = PER
    bf16, f32 = jnp.bfloat16, jnp.float32
    vmem = pl.BlockSpec(memory_space=pltpu.VMEM)
    hbm = pl.BlockSpec(memory_space=pltpu.HBM)
    dma = pltpu.SemaphoreType.DMA
    high_rows = -(-blocks // 8) * 8
    coef_shape = (chunks, lats, half, LANES)
    low_shape = (lats, BLOCK, 2 * LANES)
    high_shape = (lats, high_rows, LANES)
    message = pltpu.VMEM((chunks, n, GROUP, 2 * half), bf16)
    whole = jnp.pad(cycle_slots, (LANES, LANES - lats)) + jnp.pad(
        wave_pairs, (LANES + lats, LANES - lats - slots)
    )
    facts = whole.astype(f32) + jnp.pad(weights, (0, 2 * LANES - lat_count))
    facts = facts.reshape(1, 2 * LANES)
    field, spec_out = pl.pallas_call(
        functools.partial(fused_kernel, n, slots, lats, levels, lat_count, points),
        out_shape=(
            jax.ShapeDtypeStruct((lats, 2 * levels, points), bf16),
            jax.ShapeDtypeStruct((2, levels, rows), f32),
        ),
        in_specs=[vmem, pl.BlockSpec(memory_space=pltpu.SMEM), vmem, hbm],
        out_specs=(vmem, vmem),
        scratch_shapes=[
            pltpu.VMEM((lats, 2 * levels, points), bf16),
            pltpu.VMEM((n, 1, LANES), f32),
            pltpu.VMEM((total, rows), bf16),
            pltpu.VMEM((chunks * 2 * half, rows), bf16),
            message, message, message, message,
            pltpu.VMEM((total, lats * 2 * LANES), bf16),
            pltpu.VMEM(low_shape, bf16),
            pltpu.VMEM(high_shape, f32),
            pltpu.VMEM(high_shape, f32),
            pltpu.VMEM(coef_shape, f32),
            pltpu.VMEM((2 * half, lats * 2 * LANES), bf16),
            pltpu.VMEM((per * pairs, 2 * LANES), bf16),
            pltpu.VMEM((per * pairs, 2 * LANES), bf16),
            dma((lats,)), dma((1,)), dma((1,)),
            dma((chunks,)), dma((chunks,)), dma((chunks,)), dma((chunks,)),
        ],
        compiler_params=pltpu.CompilerParams(
            collective_id=0, has_side_effects=True,
            vmem_limit_bytes=49 * 1024 * 1024 + 512 * 1024,
        ),
    )(
        jnp.concatenate([spec_in.reshape(2 * levels, rows), legendre.T]), facts, facts,
        forcing.reshape(lats, 2 * levels, points),
    )
    return field.reshape(lats, 2, levels, points), spec_out


def solution(mesh):
    n = mesh.shape["band"]

    def run(spec_in, forcing, legendre, weights, cycle_slots, wave_pairs):
        slots = wave_pairs.shape[0]
        narrow = (
            2 * slots * n <= LANES
            and legendre.shape[1] <= LANES
            and slots * cycle_slots.shape[0] <= GROUP
            and spec_in.shape[1] % 32 == 0
        )
        args = (spec_in, forcing, legendre, weights, cycle_slots, wave_pairs)
        return on_device(n, *args) if narrow else on_device_wide(*args)

    in_specs = (
        P(None, "grp", "band"),
        P("band", None, "grp", None),
        P("band", None),
        P(),
        P("band"),
        P("band"),
    )
    out_specs = (P("band", None, "grp", None), P(None, "grp", "band"))
    return jax.shard_map(
        run, mesh=mesh, in_specs=in_specs, out_specs=out_specs, check_vma=False
    )
```

```python
import functools
import math

import jax
import jax.numpy as jnp
from jax import lax
from jax.experimental import pallas as pl
from jax.experimental.pallas import tpu as pltpu
from jax.sharding import PartitionSpec as P

TRUNC = 1279
NLON_EQ = 5136


two_pi = 2.0 * math.pi


def wave_list(pair_ids, window):
    first_wave = TRUNC + 1 - window + pair_ids
    second_wave = TRUNC - pair_ids
    return jnp.stack([first_wave, second_wave], axis=1).reshape(-1)


def fourier_table(length, wave_numbers, points):
    blocks = points // 128
    high = jnp.arange(blocks, dtype=jnp.int32) * 128
    low = jnp.arange(128, dtype=jnp.int32)
    scale = two_pi / length.astype(jnp.float32)
    angle_high = (wave_numbers[:, None] * high[None, :] % length).astype(jnp.float32) * scale
    angle_low = (wave_numbers[:, None] * low[None, :] % length).astype(jnp.float32) * scale
    cos_high = jnp.cos(angle_high)[:, :, None]
    sin_high = jnp.sin(angle_high)[:, :, None]
    cos_low = jnp.cos(angle_low)[:, None, :]
    sin_low = jnp.sin(angle_low)[:, None, :]
    count = wave_numbers.shape[0]
    cosine = (cos_high * cos_low - sin_high * sin_low).reshape(count, points)
    minus_sine = (-(sin_high * cos_low + cos_high * sin_low)).reshape(count, points)
    inside = (jnp.arange(points, dtype=jnp.int32) < length)[None, :]
    cosine = jnp.where(inside, cosine, jnp.float32(0.0))
    minus_sine = jnp.where(inside, minus_sine, jnp.float32(0.0))
    return jnp.concatenate([cosine, minus_sine], axis=0).astype(jnp.bfloat16)


def row_halves(array, axis):
    widths = [(0, 0)] * array.ndim
    widths[axis] = (0, 1)
    padded = jnp.pad(array, widths)
    shape = list(padded.shape)
    shape[axis : axis + 1] = [shape[axis] // 2, 2]
    folded = padded.reshape(shape)
    even_rows = lax.index_in_dim(folded, 0, axis + 1, keepdims=False)
    odd_rows = lax.index_in_dim(folded, 1, axis + 1, keepdims=False)
    return (even_rows, odd_rows)


def invert_rows(coefficient, legendre_rows, member, flip_sign, form):
    coef_even, coef_odd = row_halves(coefficient, 3)
    leg_even, leg_odd = row_halves(legendre_rows, 1)
    member_even, member_odd = row_halves(member, 1)
    stack_even = jnp.stack(
        [
            coef_even * (1.0 - member_even)[None, None].astype(jnp.bfloat16),
            coef_even * member_even[None, None].astype(jnp.bfloat16),
        ]
    )
    stack_odd = jnp.stack(
        [
            coef_odd * (1.0 - member_odd)[None, None].astype(jnp.bfloat16),
            coef_odd * member_odd[None, None].astype(jnp.bfloat16),
        ]
    )
    sum_even = jnp.einsum(form, stack_even, leg_even, preferred_element_type=jnp.float32)
    sum_odd = jnp.einsum(form, stack_odd, leg_odd, preferred_element_type=jnp.float32)
    north = sum_even + sum_odd
    south = (sum_even - sum_odd) * flip_sign[None, :, None, None, :]
    both = jnp.stack([north, south], axis=1)
    return jnp.transpose(both, (0, 1, 3, 4, 5, 2))


def direct_rows(combined, legendre_rows, member, flip_odd, form):
    leg_even, leg_odd = row_halves(legendre_rows, 1)
    member_even, member_odd = row_halves(member, 1)
    results = []
    for half, leg_half, member_half in ((0, leg_even, member_even), (1, leg_odd, member_odd)):
        first_part = combined[half, :, :, :, :, 0]
        second_part = jnp.where(
            flip_odd[None, None, None, :],
            combined[1 - half, :, :, :, :, 1],
            combined[half, :, :, :, :, 1],
        )
        stacked = jnp.stack([first_part, second_part])
        values = jnp.einsum(form, stacked, leg_half, preferred_element_type=jnp.float32)
        results.append(jnp.where(member_half[None, None] > 0.5, values[1], values[0]))
    merged = jnp.stack(results, axis=-1)
    shape = merged.shape
    merged = merged.reshape(shape[0], shape[1], shape[2], shape[3] * 2)
    return merged[:, :, :, : legendre_rows.shape[1]]


def on_device_wide(spec_in, forcing, legendre, weights, cycle_slots, wave_pairs):
    all_cycles, all_pairs = (
        lax.all_gather(cycle_slots, "band", axis=0, tiled=True),
        lax.all_gather(wave_pairs, "band", axis=0, tiled=True),
    )
    devices = lax.axis_size("band")
    slot_local = wave_pairs.shape[0]
    window = 2 * slot_local * devices
    row_count = window + 1
    level_count = spec_in.shape[1]
    lat_local = cycle_slots.shape[0]
    lat_count = all_cycles.shape[0]
    points = forcing.shape[3]
    offsets = jnp.arange(row_count, dtype=jnp.int32)[None, :]
    boundary = window - wave_pairs
    member = (offsets >= boundary[:, None]).astype(jnp.float32)
    flip_odd = boundary % 2 == 1
    flip_sign = jnp.stack(
        [jnp.ones((slot_local,), jnp.float32), jnp.where(flip_odd, -1.0, 1.0).astype(jnp.float32)]
    )
    coefficient = spec_in.reshape(2, level_count, slot_local, row_count)
    legendre_local = legendre.reshape(slot_local, row_count, lat_count)
    legendre_order = jnp.take(legendre_local, all_cycles, axis=2)
    fourier = invert_rows(
        coefficient, legendre_order, member, flip_sign, "welsr,srq->qwles"
    ).astype(jnp.bfloat16)
    received = lax.all_to_all(fourier, "band", split_axis=0, concat_axis=4, tiled=True)
    received = received.reshape(lat_local, 2 * level_count, 2 * window)
    wave_numbers = wave_list(all_pairs, window)
    lengths = NLON_EQ - 4 * cycle_slots
    force_rows = forcing.reshape(lat_local, 2 * level_count, points)

    def cycle_step(packed):
        fourier_cycle, force_cycle, length = packed
        dft_table = fourier_table(length, wave_numbers, points)
        field_rows = 2.0 * jnp.dot(fourier_cycle, dft_table, preferred_element_type=jnp.float32)
        product = (field_rows * force_cycle.astype(jnp.float32)).astype(jnp.bfloat16)
        returned = lax.dot_general(
            product, dft_table, (((1,), (1,)), ((), ())), preferred_element_type=jnp.float32
        )
        return (field_rows.astype(jnp.bfloat16), returned.astype(jnp.bfloat16))

    fields, returned = lax.map(cycle_step, (received, force_rows, lengths))
    grid_field = fields.reshape(lat_local, 2, level_count, points)
    returned = returned.reshape(lat_local, 2, level_count, 2, window // 2, 2)
    gathered = lax.all_to_all(returned, "band", split_axis=4, concat_axis=0, tiled=True).astype(
        jnp.float32
    )
    north_part = gathered[:, 0]
    south_part = gathered[:, 1]
    lat_weight = jnp.take(weights, all_cycles)[:, None, None, None, None]
    combined = jnp.stack(
        [lat_weight * (north_part + south_part), lat_weight * (north_part - south_part)]
    ).astype(jnp.bfloat16)
    spectral = direct_rows(combined, legendre_order, member, flip_odd, "wqles,srq->wlesr")
    spec_out = jnp.transpose(spectral, (1, 0, 2, 3)).reshape(2, level_count, slot_local * row_count)
    return (grid_field, spec_out)


MESH = pl.DeviceIdType.MESH
BLOCK = 256
GROUP = 16
CHUNKS = 1
PER = 21
LANES = 128


def unit_circle(steps, length, inverse):
    turns = jnp.floor(steps * inverse + 0.5)
    z = (steps - turns * length) * (inverse * math.pi)
    y = z * z
    s = -1.0 / 39916800.0
    for c in (1.0 / 362880.0, -1.0 / 5040.0, 1.0 / 120.0, -1.0 / 6.0, 1.0):
        s = s * y + c
    s = s * z
    k = 1.0 / 479001600.0
    for c in (-1.0 / 3628800.0, 1.0 / 40320.0, -1.0 / 720.0, 1.0 / 24.0, -0.5, 1.0):
        k = k * y + c
    return 1.0 - 2.0 * s * s, 2.0 * s * k


def fused_kernel(
    n, slots, lats, levels, lat_count, points,
    table_ref, facts_ref, weights_ref, force_hbm,
    field_v, out_ref,
    force_v, info, legm, coefm, send1, recv1, send2, recv2,
    pick, low, high_c, high_s, coef_z, back_z, twisted, prod,
    force_sem, info_ss, info_rs, f_ss, f_rs, b_ss, b_rs,
):
    window = 2 * slots * n
    row_count = window + 1
    rows = slots * row_count
    base = TRUNC + 1 - window
    chunks = send1.shape[0]
    part_levels = levels // chunks
    pairs = 2 * part_levels
    half = 2 * pairs
    blocks = -(-points // BLOCK)
    whole = (NLON_EQ - 4 * (lat_count - 1)) // BLOCK
    f32, bf16, i32 = jnp.float32, jnp.bfloat16, jnp.int32
    me = lax.axis_index("band")
    part = lax.axis_index("grp")

    def force_copy(q):
        return pltpu.make_async_copy(force_hbm.at[q], force_v.at[q], force_sem.at[q])

    def cycle(q):
        return facts_ref[0, LANES + q]

    def pair(s):
        return facts_ref[0, LANES + lats + s]

    barrier = pltpu.get_barrier_semaphore()

    def peer(i):
        return lax.rem(me + i, n)

    @pl.loop(1, n, unroll=n - 1)
    def _(i):
        pl.semaphore_signal(barrier, inc=1, device_id=(part, peer(i)), device_id_type=MESH)

    for q in range(lats):
        force_copy(q).start()

    lane1 = lax.broadcasted_iota(i32, (1, LANES), 1)
    mine = jnp.full((1, LANES), -1.0, f32)
    for q in range(lats):
        for s in range(slots):
            k = q * slots + s
            mine = jnp.where(lane1 == k, cycle(q), mine)
            mine = jnp.where(lane1 == GROUP + k, pair(s), mine)
    info[me] = mine

    def remote(src, dst, ssem, rsem, to):
        return pltpu.make_async_remote_copy(
            src_ref=src, dst_ref=dst, send_sem=ssem, recv_sem=rsem,
            device_id=(part, to), device_id_type=MESH,
        )

    def all_of(buffer, sem):
        others = buffer.at[pl.ds(0, n - 1)]
        return pltpu.make_async_copy(others, others, sem)

    pl.semaphore_wait(barrier, n - 1)

    @pl.loop(1, n, unroll=n - 1)
    def _(i):
        remote(info.at[me], info.at[me], info_ss.at[0], info_rs.at[0], peer(i)).start()

    @pl.loop(0, lats)
    def _(q):
        length = jnp.full((1, LANES), NLON_EQ - 4.0 * cycle(q), f32)
        inverse = 1.0 / length
        m_low = base + lax.broadcasted_iota(i32, (BLOCK, LANES), 1)
        v_low = lax.broadcasted_iota(i32, (BLOCK, LANES), 0)
        c, s = unit_circle((m_low * v_low).astype(f32), length, inverse)
        low[q, :, 0:LANES] = c.astype(bf16)
        low[q, :, LANES : 2 * LANES] = s.astype(bf16)
        height = high_c.shape[1]
        m_high = base + lax.broadcasted_iota(i32, (height, LANES), 1)
        u_high = lax.broadcasted_iota(i32, (height, LANES), 0) * BLOCK
        c, s = unit_circle((m_high * u_high).astype(f32), length, inverse)
        high_c[q] = c
        high_s[q] = s

    lane = lax.broadcasted_iota(i32, (1, rows), 1).astype(f32)
    offset = lane
    boundary = jnp.full((1, rows), window - pair(0), f32)
    for s in range(1, slots):
        here = lane >= s * row_count
        offset = jnp.where(here, lane - s * row_count, offset)
        boundary = jnp.where(here, window - pair(s), boundary)
    second = offset >= boundary
    degree = jnp.where(second, offset - boundary, offset)
    odd = degree - 2.0 * jnp.floor(0.5 * degree) > 0.5
    in_wave = [jnp.where(second, 0.0, 1.0), jnp.where(second, 1.0, 0.0)]
    sign = jnp.where(odd, -1.0, 1.0)
    for e in range(2):
        values = table_ref[e * levels : (e + 1) * levels].astype(f32)
        for w in range(2):
            north = values * in_wave[w]
            south = north * sign
            for c in range(chunks):
                at = c * 2 * half + (w * 2 + e) * pairs
                take = slice(c * part_levels, (c + 1) * part_levels)
                coefm[at : at + part_levels, :] = north[take].astype(bf16)
                coefm[at + part_levels : at + pairs, :] = south[take].astype(bf16)
    back_z[...] = jnp.zeros_like(back_z)
    all_of(info, info_rs.at[0]).wait()

    total = n * GROUP
    gathered = jnp.broadcast_to(info[...], (n, GROUP, LANES)).reshape(total, LANES)
    lane_all = lax.broadcasted_iota(i32, (total, LANES), 1)
    place_all = lax.broadcasted_iota(i32, (total, LANES), 0) & (GROUP - 1)

    def column(first):
        here = lane_all == place_all + first
        return jnp.sum(jnp.where(here, gathered, 0.0), axis=1, keepdims=True).astype(i32)

    cycles = column(0)
    waves = column(GROUP)
    hot = jnp.where(cycles == lax.broadcasted_iota(i32, (total, LANES), 1), 1.0, 0.0)
    leg_all = lax.dot_general(
        hot[:, :lat_count].astype(bf16), table_ref[2 * levels : 2 * levels + lat_count], (((1,), (0,)), ((), ())),
        preferred_element_type=f32,
    )

    def row_lat(width):
        place = lax.broadcasted_iota(i32, (total, width), 0) & (GROUP - 1)
        lat = jnp.zeros((total, width), i32)
        for k in range(1, GROUP // slots + 1):
            lat = lat + jnp.where(place >= k * slots, 1, 0)
        return lat, place - lat * slots

    _, slot_of = row_lat(rows)
    lane_full = lax.broadcasted_iota(i32, (total, rows), 1) - slot_of * row_count
    keep = (lane_full >= 0) & (lane_full < row_count)
    legm[...] = jnp.where(keep, leg_all, 0.0).astype(bf16)
    fourier = lax.dot_general(
        legm[...], coefm[...], (((1,), (1,)), ((), ())), preferred_element_type=f32
    ).astype(bf16)
    for c in range(chunks):
        send1[c] = fourier[:, c * 2 * half : (c + 1) * 2 * half].reshape(n, GROUP, 2 * half)

    for c in range(chunks):

        @pl.loop(1, n, unroll=n - 1)
        def _(i):
            to = peer(i)
            remote(send1.at[c, to], recv1.at[c, me], f_ss.at[c], f_rs.at[c], to).start()

        recv1[c, me] = send1[c, me]

    lat_of, _ = row_lat(LANES)
    for q in range(lats):
        here = lat_of == q
        at = q * 2 * LANES
        pick[:, at : at + LANES] = jnp.where(here & (lane_all == waves), 1.0, 0.0).astype(bf16)
        pick[:, at + LANES : at + 2 * LANES] = jnp.where(
            here & (lane_all == window - 1 - waves), 1.0, 0.0
        ).astype(bf16)

    per = twisted.shape[0] // pairs
    for c in range(chunks):

        all_of(recv1.at[c], f_rs.at[c]).wait()

        arrived = recv1[c].reshape(total, 2 * half)
        both = lax.dot_general(
            arrived, pick[...], (((0,), (0,)), ((), ())), preferred_element_type=f32
        )
        for q in range(lats):
            at = q * 2 * LANES
            coef_z[c, q] = 2.0 * (
                both[0:half, at : at + LANES] + both[half : 2 * half, at + LANES : at + 2 * LANES]
            )

        @pl.loop(0, lats)
        def _(q):
            if c == 0:
                force_copy(q).wait()
            length = NLON_EQ - 4.0 * cycle(q)
            acc_re = jnp.zeros((pairs, LANES), f32)
            acc_im = jnp.zeros((pairs, LANES), f32)
            for first in range(0, blocks, per):
                count = min(per, blocks - first)
                fields = low_sums(coef_z, high_c, high_s, low, twisted, (c, q), q, pairs, first, count)
                for k in range(count):
                    u = first + k
                    width = min(BLOCK, points - u * BLOCK)
                    f = inside(fields[k * pairs : (k + 1) * pairs, 0:width], u, whole, length)
                    cols = slice(u * BLOCK, u * BLOCK + width)
                    for h in range(2):
                        rows_h = slice(h * levels + c * part_levels, h * levels + (c + 1) * part_levels)
                        at = k * pairs + h * part_levels
                        fh = f[h * part_levels : (h + 1) * part_levels]
                        field_v[q, rows_h, cols] = fh.astype(bf16)
                        p = fh * force_v[q, rows_h, cols].astype(f32)
                        prod[at : at + part_levels, 0:width] = p.astype(bf16)
                    if width < BLOCK:
                        prod[k * pairs : (k + 1) * pairs, width:BLOCK] = jnp.zeros(
                            (pairs, BLOCK - width), bf16
                        )
                back = jnp.dot(prod[0 : count * pairs], low[q], preferred_element_type=f32)
                for k in range(count):
                    u = first + k
                    hc = high_c[q, u : u + 1, :]
                    hs = high_s[q, u : u + 1, :]
                    tc = back[k * pairs : (k + 1) * pairs, 0:LANES]
                    ts = back[k * pairs : (k + 1) * pairs, LANES : 2 * LANES]
                    acc_re = acc_re + (tc * hc - ts * hs)
                    acc_im = acc_im - (tc * hs + ts * hc)
            mine = lax.broadcasted_iota(i32, (1, LANES), 1).astype(f32) == cycle(q)
            weight = jnp.sum(
                jnp.where(mine, weights_ref[:, 0:LANES], 0.0), axis=1, keepdims=True
            )
            for e, acc in ((0, acc_re), (1, acc_im)):
                rounded = acc.astype(bf16).astype(f32)
                north = rounded[0:part_levels]
                south = rounded[part_levels:pairs]
                for g, value in ((0, north + south), (1, north - south)):
                    value = (weight * value).astype(bf16)
                    for w in range(2):
                        at = w * half + e * pairs + g * part_levels
                        lane_at = pl.multiple_of(q * 2 * LANES + w * LANES, LANES)
                        back_z[at : at + part_levels, pl.ds(lane_at, LANES)] = value

        z = lax.dot_general(
            pick[...], back_z[...], (((1,), (1,)), ((), ())), preferred_element_type=f32
        )
        send2[c] = z.astype(bf16).reshape(n, GROUP, 2 * half)

        @pl.loop(1, n, unroll=n - 1)
        def _(i):
            to = peer(i)
            remote(send2.at[c, to], recv2.at[c, me], b_ss.at[c], b_rs.at[c], to).start()

        recv2[c, me] = send2[c, me]

    for c in range(chunks):

        all_of(recv2.at[c], b_rs.at[c]).wait()

        final = lax.dot_general(
            recv2[c].reshape(total, 2 * half), legm[...], (((0,), (0,)), ((), ())),
            preferred_element_type=f32,
        )
        for e in range(2):
            chosen = []
            for w in range(2):
                at = (w * 2 + e) * pairs
                chosen.append(
                    jnp.where(odd, final[at + part_levels : at + pairs], final[at : at + part_levels])
                )
            out_ref[e, c * part_levels : (c + 1) * part_levels] = jnp.where(second, chosen[1], chosen[0])

    all_of(info, info_ss.at[0]).wait()
    for c in range(chunks):
        all_of(send1.at[c], f_ss.at[c]).wait()
        all_of(send2.at[c], b_ss.at[c]).wait()


def low_sums(coef_z, high_c, high_s, low, twisted, at, q, pairs, first, count):
    real = coef_z[at[0], at[1], 0:pairs]
    imag = coef_z[at[0], at[1], pairs : 2 * pairs]
    for k in range(count):
        hc = high_c[q, first + k : first + k + 1, :]
        hs = high_s[q, first + k : first + k + 1, :]
        rows = slice(k * pairs, (k + 1) * pairs)
        twisted[rows, 0:LANES] = (real * hc - imag * hs).astype(jnp.bfloat16)
        twisted[rows, LANES : 2 * LANES] = (-(real * hs + imag * hc)).astype(jnp.bfloat16)
    return lax.dot_general(
        twisted[0 : count * pairs], low[q], (((1,), (1,)), ((), ())),
        preferred_element_type=jnp.float32,
    )


def inside(f, u, whole, length):
    if u < whole:
        return f
    j = u * BLOCK + lax.broadcasted_iota(jnp.int32, f.shape, 1)
    return jnp.where(j.astype(jnp.float32) < length, f, 0.0)


def on_device(n, spec_in, forcing, legendre, weights, cycle_slots, wave_pairs):
    slots = wave_pairs.shape[0]
    lats = cycle_slots.shape[0]
    levels = spec_in.shape[1]
    rows, lat_count = legendre.shape
    points = forcing.shape[3]
    chunks = CHUNKS
    pairs = 2 * levels // chunks
    half = 2 * pairs
    total = n * GROUP
    blocks = -(-points // BLOCK)
    per = PER
    bf16, f32 = jnp.bfloat16, jnp.float32
    vmem = pl.BlockSpec(memory_space=pltpu.VMEM)
    hbm = pl.BlockSpec(memory_space=pltpu.HBM)
    dma = pltpu.SemaphoreType.DMA
    high_rows = -(-blocks // 8) * 8
    coef_shape = (chunks, lats, half, LANES)
    low_shape = (lats, BLOCK, 2 * LANES)
    high_shape = (lats, high_rows, LANES)
    message = pltpu.VMEM((chunks, n, GROUP, 2 * half), bf16)
    whole = jnp.pad(cycle_slots, (LANES, LANES - lats)) + jnp.pad(
        wave_pairs, (LANES + lats, LANES - lats - slots)
    )
    facts = whole.astype(f32) + jnp.pad(weights, (0, 2 * LANES - lat_count))
    facts = facts.reshape(1, 2 * LANES)
    field, spec_out = pl.pallas_call(
        functools.partial(fused_kernel, n, slots, lats, levels, lat_count, points),
        out_shape=(
            jax.ShapeDtypeStruct((lats, 2 * levels, points), bf16),
            jax.ShapeDtypeStruct((2, levels, rows), f32),
        ),
        in_specs=[vmem, pl.BlockSpec(memory_space=pltpu.SMEM), vmem, hbm],
        out_specs=(vmem, vmem),
        scratch_shapes=[
            pltpu.VMEM((lats, 2 * levels, points), bf16),
            pltpu.VMEM((n, 1, LANES), f32),
            pltpu.VMEM((total, rows), bf16),
            pltpu.VMEM((chunks * 2 * half, rows), bf16),
            message, message, message, message,
            pltpu.VMEM((total, lats * 2 * LANES), bf16),
            pltpu.VMEM(low_shape, bf16),
            pltpu.VMEM(high_shape, f32),
            pltpu.VMEM(high_shape, f32),
            pltpu.VMEM(coef_shape, f32),
            pltpu.VMEM((2 * half, lats * 2 * LANES), bf16),
            pltpu.VMEM((per * pairs, 2 * LANES), bf16),
            pltpu.VMEM((per * pairs, 2 * LANES), bf16),
            dma((lats,)), dma((1,)), dma((1,)),
            dma((chunks,)), dma((chunks,)), dma((chunks,)), dma((chunks,)),
        ],
        compiler_params=pltpu.CompilerParams(
            collective_id=0, has_side_effects=True,
            vmem_limit_bytes=49 * 1024 * 1024 + 512 * 1024,
        ),
    )(
        jnp.concatenate([spec_in.reshape(2 * levels, rows), legendre.T]), facts, facts,
        forcing.reshape(lats, 2 * levels, points),
    )
    return field.reshape(lats, 2, levels, points), spec_out


def solution(mesh):
    n = mesh.shape["band"]

    def run(spec_in, forcing, legendre, weights, cycle_slots, wave_pairs):
        slots = wave_pairs.shape[0]
        narrow = (
            2 * slots * n <= LANES
            and legendre.shape[1] <= LANES
            and slots * cycle_slots.shape[0] <= GROUP
            and spec_in.shape[1] % 32 == 0
        )
        args = (spec_in, forcing, legendre, weights, cycle_slots, wave_pairs)
        return on_device(n, *args) if narrow else on_device_wide(*args)

    in_specs = (
        P(None, "grp", "band"),
        P("band", None, "grp", None),
        P("band", None),
        P(),
        P("band"),
        P("band"),
    )
    out_specs = (P("band", None, "grp", None), P(None, "grp", "band"))
    return jax.shard_map(
        run, mesh=mesh, in_specs=in_specs, out_specs=out_specs, check_vma=False
    )
```
